512 devices in a mesh: dp: 32 (over y_hi, z, core), fsdp: 16 (over x, y_lo).
Axes of the slice: x: 4, y: 8 (y_hi: 2, y_lo: 4; y = y_hi * 4 + y_lo), z: 8, core: 2. Of those that a mesh axis runs over, the one named last changes fastest.
Arguments:
- inputs: bfloat16 [4096, 8192], P('fsdp', 'dp'), may hold values from -6 to 6
- cotangent: bfloat16 [4096, 14336], P('fsdp', 'dp'), may hold values from -6 to 6
- weight: bfloat16 [8192, 14336], P('dp', 'fsdp'), may hold values from -0.046875 to 0.046875
- projector: bfloat16 [8192, 512], P('dp'), may hold values from -0.25 to 0.25
- first_moment: float32 [512, 14336], P('dp', 'fsdp'), may hold values from -384 to 384
- second_moment: float32 [512, 14336], P('dp', 'fsdp'), may hold values from 327.68 to 13107.2
Outputs:
- input_grad: bfloat16 [4096, 8192], P('fsdp', 'dp')
- update: bfloat16 [8192, 14336], P('dp', 'fsdp')
The draws below stay inside these ranges and needn't reach their ends.
All inputs are finite; a program needn't handle non-finite values.
Results may differ from the reference program's by a relative error of at most 0.0052.
Values may be sent and summed in bfloat16 or wider, within the bound.
A program may use at most 64 MiB of HBM per device.

```python
import math
import jax
import jax.numpy as jnp

D = 8192
FF = 14336
RANK = 512
TOKENS = 4096


def block_scale(own_key, shape, shards, low, top_value):
    loudness, own = 1.0, jax.random.fold_in(own_key, 6)
    for position, blocks in shards:
        heights = jnp.exp(jax.random.uniform(jax.random.fold_in(own, position), (blocks,), jnp.float32, low / len(shards), top_value / len(shards)))
        loudness = loudness * jnp.repeat(heights, shape[position] // blocks).reshape([-1 if axis == position else 1 for axis in range(len(shape))])
    return loudness


def noise(own_key, extent, width, most, pieces=(), kind=jnp.bfloat16):
    loudness = block_scale(own_key, extent, pieces, -0.22, 0.18) if pieces else 1.0
    result = jax.random.normal(own_key, extent, jnp.float32) * width * loudness
    return jnp.minimum(jnp.maximum(result, -most), most).astype(kind)


def setup_inputs(seed: int = 0) -> dict:
    streams_of = jax.random.split(jax.random.key(seed), 7)
    return {
        "inputs": noise(streams_of[0], (TOKENS, D), 1.0, 6.0, ((0, 16), (1, 32))),
        "cotangent": noise(streams_of[1], (TOKENS, FF), 1.0, 6.0, ((0, 16), (1, 32))),
        "weight": noise(streams_of[2], (D, FF), FF ** -0.5, 0.046875, ((0, 32), (1, 16))),
        "projector": noise(streams_of[3], (D, RANK), RANK ** -0.5, 0.25, ((0, 32),)),
        "first_moment": noise(streams_of[4], (RANK, FF), (0.8 * TOKENS ** 0.5), 384.0, ((0, 32), (1, 16)), jnp.float32),
        "second_moment": jnp.clip(jnp.exp(math.log(13107.2) - 3.6888795 * jax.random.uniform(streams_of[5], (RANK, FF), jnp.float32) ** block_scale(streams_of[5], (RANK, FF), ((0, 32), (1, 16)), -0.2, 0.2)), 327.68, 13107.2),
    }


decay_first = 0.9
decay_second = 0.999
bias_first = 0.9999734386
bias_second = 0.0952078528
epsilon_value = 1e-08

def reference(inputs, cotangent, weight, projector, first_moment, second_moment):
    projected = jnp.dot(inputs, projector, preferred_element_type=jnp.float32).astype(jnp.bfloat16)
    gradient = jnp.dot(projected.T, cotangent, preferred_element_type=jnp.float32)
    moment_one = decay_first * first_moment + (1.0 - decay_first) * gradient
    moment_two = decay_second * second_moment + (1.0 - decay_second) * gradient * gradient
    direction = (moment_one / bias_first / (jnp.sqrt(moment_two / bias_second) + epsilon_value)).astype(jnp.bfloat16)
    update = jnp.dot(projector, direction, preferred_element_type=jnp.float32).astype(jnp.bfloat16)
    input_grad = jnp.dot(cotangent, weight.T, preferred_element_type=jnp.float32).astype(jnp.bfloat16)
    return (input_grad, update)
```

```python
import jax
import jax.numpy as jnp
from jax import lax
from jax.experimental import pallas as pl
from jax.experimental.pallas import tpu as pltpu
from jax.sharding import PartitionSpec as P

decay_first = 0.9
decay_second = 0.999
bias_first = 0.9999734386
bias_second = 0.0952078528
epsilon_value = 1e-08

MESH = pl.DeviceIdType.MESH
BF16 = jnp.bfloat16
F32 = jnp.float32

ORDER = (
    (0, 0), (0, 1), (0, 2), (0, 3), (1, 0), (0, 4), (1, 1), (0, 5),
    (1, 2), (0, 6), (1, 3), (0, 7), (1, 4), (1, 5), (1, 6), (1, 7),
)
LAG = 5
HALF = 448
PART = 224


def remote(src, dst, send, recv, device):
    return pltpu.make_async_remote_copy(
        src_ref=src,
        dst_ref=dst,
        send_sem=send,
        recv_sem=recv,
        device_id=device,
        device_id_type=MESH,
    )


def landed(ref, sem):
    pltpu.make_async_copy(ref, ref, sem).wait()


def kernel(
    inputs, cotangent, weight, projector, first, second, grad_out, update_out,
    ring, blocks, weights, total, grads, part, part_in, pair, half_out, half_in, shares, shares_in, projected,
    grads_out, grads_in, sums_out, sums_in, direction,
    h_send, ring_recv, ring_send, x_send, x_recv, sib_send, sib_recv, w_send, w_recv,
    p_send, p_recv, ph_send, ph_recv, pz_send, pz_recv, px_send, px_recv,
    g_send, g_recv, c_send, c_recv, dh_send, d_recv, d_send, ds_send, ds_recv,
):
    j = lax.axis_index("dp")
    i = lax.axis_index("fsdp")
    x, l = i // 4, i % 4
    h, z, c = j // 16, (j // 2) % 8, j % 2

    def at(x=x, l=l, h=h, z=z, c=c):
        return {"dp": h * 16 + z * 2 + c, "fsdp": x * 4 + l}

    sibling = at(c=1 - c)
    partner = at(h=1 - h)
    right, left = at(z=(z + 1) % 8), at(z=(z + 7) % 8)

    barrier = pltpu.get_barrier_semaphore()
    peers = [sibling, partner]
    peers += [at(z=(z + k) % 8) for k in range(1, 8)]
    peers += [at(x=(x + k) % 4) for k in range(1, 4)]
    peers += [at(l=(l + k) % 4) for k in range(1, 4)]
    for peer in peers:
        pl.semaphore_signal(barrier, inc=1, device_id=peer, device_id_type=MESH)
    ring[0, z] = cotangent[...]
    weights[l] = weight[...]
    total[...] = jnp.zeros_like(total)
    grads[...] = jnp.zeros_like(grads)
    pl.semaphore_wait(barrier, len(peers))

    for s in range(2):
        rows = pl.ds(s * PART, PART)
        remote(ring.at[0, z, rows], ring.at[1, z, rows], h_send.at[s], ring_recv.at[1, z, s], partner).start()

    def place(q, o):
        dist = (o + 1) // 2
        zf = (z + 8 - dist) % 8 if o % 2 else (z + dist) % 8
        hf = h if q == 0 else 1 - h
        return dist, zf, 2 * hf + zf // 4, zf % 4

    def relay(q, o):
        dist, zf, xf, lf = place(q, o)
        for s in range(2):
            rows = pl.ds(s * PART, PART)
            piece = ring.at[q, zf, rows]
            if (q, o) != (0, 0):
                landed(piece, ring_recv.at[q, zf, s])
            if o == 0 or (o % 2 == 1 and dist + 1 <= 4 - s):
                remote(piece, piece, ring_send.at[q, 0, dist, s], ring_recv.at[q, zf, s], right).start()
            if o == 0 or (o % 2 == 0 and dist + 1 <= 3 + s):
                remote(piece, piece, ring_send.at[q, 1, dist, s], ring_recv.at[q, zf, s], left).start()

            @pl.when(xf != x)
            def _():
                there = blocks.at[lf, x, pl.ds(c * HALF + s * PART, PART)]
                remote(piece, there, x_send.at[q, o, s], x_recv.at[lf, x, s], at(x=xf)).start()

        @pl.when(xf == x)
        def _():
            there = blocks.at[lf, x, pl.ds(c * HALF, HALF)]
            remote(ring.at[q, zf], there, sib_send.at[lf, x], sib_recv.at[lf, x], sibling).start()
            blocks[lf, x, pl.ds(c * HALF, HALF)] = ring[q, zf]

    def share(q, o):
        _, _, xf, lf = place(q, o)

        @pl.when(xf == x)
        def _():
            for k in range(1, 4):
                xt = (x + k) % 4
                for s in range(2):
                    landed(blocks.at[lf, xt, pl.ds(c * HALF + s * PART, PART)], x_recv.at[lf, xt, s])
                mine = blocks.at[lf, xt, pl.ds(c * HALF, HALF)]
                remote(mine, mine, sib_send.at[lf, xt], sib_recv.at[lf, xt], sibling).start()

    def send_weight(origin, way):
        block = weights.at[origin]
        target = at(l=l + 1) if way == 0 else at(l=l - 1)
        return remote(block, block, w_send.at[way, origin], w_recv.at[origin], target)

    def pass_weight(step):
        @pl.when(l >= step)
        def _():
            if step:
                landed(weights.at[l - step], w_recv.at[l - step])

            @pl.when(l < 3)
            def _():
                send_weight(l - step, 0).start()

        @pl.when(l + step <= 3)
        def _():
            if step:
                landed(weights.at[l + step], w_recv.at[l + step])

            @pl.when(l > 0)
            def _():
                send_weight(l + step, 1).start()

    def project_pair():
        product = jnp.dot(inputs[...], projector[...], preferred_element_type=F32)
        part[...] = product.T.reshape(part.shape)
        remote(part.at[:, :, 1 - c], part_in, p_send, p_recv, sibling).start()

    def project_half():
        landed(part_in, p_recv)
        pair[...] = part[:, :, c] + part_in[...]
        half_out[...] = pair[1 - h].astype(BF16)
        remote(half_out, half_in, ph_send, ph_recv, partner).start()

    def project_share():
        landed(half_in, ph_recv)
        pair[h] = pair[h] + half_in[...].astype(F32)
        shares[...] = pair[h].astype(BF16)
        for k in range(1, 8):
            zp = (z + k) % 8
            remote(shares.at[zp], shares_in.at[z], pz_send.at[zp], pz_recv.at[z], at(z=zp)).start()

    def project_own():
        own = pair[h, z]
        for k in range(1, 8):
            zp = (z + k) % 8
            landed(shares_in.at[zp], pz_recv.at[zp])
            own = own + shares_in[zp].astype(F32)
        projected[x] = own.astype(BF16)
        for k in range(1, 4):
            xp = (x + k) % 4
            remote(projected.at[x], projected.at[x], px_send.at[xp], px_recv.at[x], at(x=xp)).start()

    for n, (q, o) in enumerate(ORDER):
        relay(q, o)
        if n >= LAG:
            share(*ORDER[n - LAG])
        if n == 0:
            project_pair()
        if n == 1:
            pass_weight(0)
            project_half()
        if n == 4:
            project_share()
        if n == 6:
            project_own()
            pass_weight(1)
        if n == 11:
            pass_weight(2)
    for n in range(16 - LAG, 16):
        share(*ORDER[n])

    @pl.when(l == 3)
    def _():
        landed(weights.at[0], w_recv.at[0])

    @pl.when(l == 0)
    def _():
        landed(weights.at[3], w_recv.at[3])

    for k in range(1, 4):
        xp = (x + k) % 4
        landed(projected.at[xp], px_recv.at[xp])

    def multiply(n, carry):
        lf, xt = n // 4, n % 4
        landed(blocks.at[lf, xt, pl.ds((1 - c) * HALF, HALF)], sib_recv.at[lf, xt])
        block = blocks[lf, xt]
        total[xt] += jnp.dot(weights[lf], block, preferred_element_type=F32)
        grads[lf] += lax.dot_general(
            projected[xt], block, (((1,), (1,)), ((), ())), preferred_element_type=F32
        )
        return carry

    lax.fori_loop(0, 16, multiply, 0)

    for k in range(1, 4):
        lp = (l + k) % 4
        grads_out[lp] = grads[lp].astype(BF16)
        remote(grads_out.at[lp], grads_in.at[l], g_send.at[lp], g_recv.at[l], at(l=lp)).start()
    for k in range(1, 4):
        xp = (x + k) % 4
        sums_out[xp] = total[xp].astype(BF16)
        remote(sums_out.at[xp], sums_in.at[x], c_send.at[xp], c_recv.at[x], at(x=xp)).start()

    gradient = grads[l]
    for k in range(1, 4):
        lp = (l + k) % 4
        landed(grads_in.at[lp], g_recv.at[lp])
        gradient = gradient + grads_in[lp].astype(F32)
    moment_one = decay_first * first[...] + (1.0 - decay_first) * gradient
    moment_two = decay_second * second[...] + (1.0 - decay_second) * gradient * gradient
    direction[h, z, c] = (
        moment_one / bias_first / (jnp.sqrt(moment_two / bias_second) + epsilon_value)
    ).astype(BF16)

    mine = direction.at[h, z, c]
    remote(mine, mine, dh_send, d_recv.at[1, z], partner).start()
    for q, o in ORDER:
        dist, zf, _, _ = place(q, o)
        hf = h if q == 0 else 1 - h
        piece = direction.at[hf, zf, c]
        if (q, o) != (0, 0):
            landed(piece, d_recv.at[q, zf])
        if o == 0 or (o % 2 == 1 and dist + 1 <= 4 - q):
            remote(piece, piece, d_send.at[q, 0, dist], d_recv.at[q, zf], right).start()
        if o == 0 or (o % 2 == 0 and dist + 1 <= 3 + q):
            remote(piece, piece, d_send.at[q, 1, dist], d_recv.at[q, zf], left).start()
    both = direction.at[:, :, c]
    remote(both, both, ds_send, ds_recv, sibling).start()

    result = total[x]
    for k in range(1, 4):
        xp = (x + k) % 4
        landed(sums_in.at[xp], c_recv.at[xp])
        result = result + sums_in[xp].astype(F32)
    grad_out[...] = result.T.astype(BF16)

    landed(direction.at[:, :, 1 - c], ds_recv)
    update_out[...] = jnp.dot(
        projector[...], direction[...].reshape(512, 896), preferred_element_type=F32
    ).astype(BF16)

    for s in range(2):
        landed(ring.at[0, z, pl.ds(s * PART, PART)], h_send.at[s])
    for q, o in ORDER:
        dist, zf, xf, lf = place(q, o)
        for s in range(2):
            piece = ring.at[q, zf, pl.ds(s * PART, PART)]
            if o == 0 or (o % 2 == 1 and dist + 1 <= 4 - s):
                landed(piece, ring_send.at[q, 0, dist, s])
            if o == 0 or (o % 2 == 0 and dist + 1 <= 3 + s):
                landed(piece, ring_send.at[q, 1, dist, s])

            @pl.when(xf != x)
            def _():
                landed(piece, x_send.at[q, o, s])

        if o == 0 or (o % 2 == 1 and dist + 1 <= 4 - q):
            landed(direction.at[h, zf, c], d_send.at[q, 0, dist])
        if o == 0 or (o % 2 == 0 and dist + 1 <= 3 + q):
            landed(direction.at[h, zf, c], d_send.at[q, 1, dist])
    for lf in range(4):
        for xt in range(4):
            landed(blocks.at[lf, xt, pl.ds(c * HALF, HALF)], sib_send.at[lf, xt])
    for step in range(3):

        @pl.when((l >= step) & (l < 3))
        def _():
            send_weight(l - step, 0).wait_send()

        @pl.when((l + step <= 3) & (l > 0))
        def _():
            send_weight(l + step, 1).wait_send()

    landed(part_in, p_send)
    landed(half_out, ph_send)
    for k in range(1, 8):
        zp = (z + k) % 8
        landed(shares.at[zp], pz_send.at[zp])
    for k in range(1, 4):
        xp, lp = (x + k) % 4, (l + k) % 4
        landed(projected.at[x], px_send.at[xp])
        landed(grads_out.at[lp], g_send.at[lp])
        landed(sums_out.at[xp], c_send.at[xp])
    landed(mine, dh_send)
    landed(both, ds_send)


def body(inputs, cotangent, weight, projector, first_moment, second_moment):
    dma = pltpu.SemaphoreType.DMA
    vmem = pl.BlockSpec(memory_space=pltpu.VMEM)
    return pl.pallas_call(
        kernel,
        out_shape=(
            jax.ShapeDtypeStruct((256, 256), BF16),
            jax.ShapeDtypeStruct((256, 896), BF16),
        ),
        in_specs=[vmem] * 6,
        out_specs=(vmem, vmem),
        scratch_shapes=[
            pltpu.VMEM((2, 8, 448, 256), BF16),
            pltpu.VMEM((4, 4, 896, 256), BF16),
            pltpu.VMEM((4, 256, 896), BF16),
            pltpu.VMEM((4, 256, 256), F32),
            pltpu.VMEM((4, 16, 896), F32),
            pltpu.VMEM((2, 8, 2, 16, 256), F32),
            pltpu.VMEM((2, 8, 16, 256), F32),
            pltpu.VMEM((2, 8, 16, 256), F32),
            pltpu.VMEM((8, 16, 256), BF16),
            pltpu.VMEM((8, 16, 256), BF16),
            pltpu.VMEM((8, 16, 256), BF16),
            pltpu.VMEM((8, 16, 256), BF16),
            pltpu.VMEM((4, 16, 256), BF16),
            pltpu.VMEM((4, 16, 896), BF16),
            pltpu.VMEM((4, 16, 896), BF16),
            pltpu.VMEM((4, 256, 256), BF16),
            pltpu.VMEM((4, 256, 256), BF16),
            pltpu.VMEM((2, 8, 2, 16, 896), BF16),
            dma((2,)), dma((2, 8, 2)), dma((2, 2, 4, 2)), dma((2, 8, 2)), dma((4, 4, 2)),
            dma((4, 4)), dma((4, 4)), dma((2, 4)), dma((4,)),
            dma(()), dma(()), dma(()), dma(()), dma((8,)), dma((8,)), dma((4,)), dma((4,)),
            dma((4,)), dma((4,)), dma((4,)), dma((4,)), dma(()), dma((2, 8)), dma((2, 2, 4)), dma(()), dma(()),
        ],
        compiler_params=pltpu.CompilerParams(
            collective_id=0, has_side_effects=True, vmem_limit_bytes=48 * 2**20
        ),
        cost_estimate=pl.CostEstimate(
            flops=2_300_000_000, bytes_accessed=2_000_000, transcendentals=28_672
        ),
        name="step",
    )(inputs, cotangent.T, weight, projector, first_moment, second_moment)


def solution(mesh):
    return jax.shard_map(
        body,
        mesh=mesh,
        in_specs=(
            P("fsdp", "dp"),
            P("fsdp", "dp"),
            P("dp", "fsdp"),
            P("dp", None),
            P("dp", "fsdp"),
            P("dp", "fsdp"),
        ),
        out_specs=(P("fsdp", "dp"), P("dp", "fsdp")),
        check_vma=False,
    )
```

```python
import jax
import jax.numpy as jnp
from jax import lax
from jax.experimental import pallas as pl
from jax.experimental.pallas import tpu as pltpu
from jax.sharding import PartitionSpec as P

decay_first = 0.9
decay_second = 0.999
bias_first = 0.9999734386
bias_second = 0.0952078528
epsilon_value = 1e-08

MESH = pl.DeviceIdType.MESH
BF16 = jnp.bfloat16
F32 = jnp.float32

ORDER = (
    (0, 0), (0, 1), (0, 2), (1, 0), (0, 3), (1, 1), (0, 4), (1, 2),
    (0, 5), (1, 3), (0, 6), (1, 4), (0, 7), (1, 5), (1, 6), (1, 7),
)
HALF = 448
PART = 224


def remote(src, dst, send, recv, device):
    return pltpu.make_async_remote_copy(
        src_ref=src,
        dst_ref=dst,
        send_sem=send,
        recv_sem=recv,
        device_id=device,
        device_id_type=MESH,
    )


def landed(ref, sem):
    pltpu.make_async_copy(ref, ref, sem).wait()


def kernel(
    inputs_hbm, cotangent_hbm, weight_hbm, projector_hbm, first_hbm, second_hbm, grad_out, update_out,
    inputs, projector, first, second, ring, blocks, weights, total, grads, part, part_in, pair, half_out, half_in, shares, shares_in, projected,
    grads_out, grads_in, sums_out, sums_in, direction,
    load, h_send, ring_recv, ring_send, x_send, x_recv, sib_send, sib_recv, w_send, w_recv,
    p_send, p_recv, ph_send, ph_recv, pz_send, pz_recv, px_send, px_recv,
    g_send, g_recv, c_send, c_recv, dh_send, d_recv, d_send, ds_send, ds_recv,
):
    j = lax.axis_index("dp")
    i = lax.axis_index("fsdp")
    x, l = i // 4, i % 4
    h, z, c = j // 16, (j // 2) % 8, j % 2

    def at(x=x, l=l, h=h, z=z, c=c):
        return {"dp": h * 16 + z * 2 + c, "fsdp": x * 4 + l}

    sibling = at(c=1 - c)
    partner = at(h=1 - h)
    right, left = at(z=(z + 1) % 8), at(z=(z + 7) % 8)

    def fetch(n):
        src, dst = (
            (cotangent_hbm, ring.at[0, z]), (inputs_hbm, inputs), (projector_hbm, projector),
            (weight_hbm, weights.at[l]), (first_hbm, first), (second_hbm, second),
        )[n]
        return pltpu.make_async_copy(src, dst, load.at[n])

    barrier = pltpu.get_barrier_semaphore()
    peers = [sibling, partner]
    peers += [at(z=(z + k) % 8) for k in range(1, 8)]
    peers += [at(x=(x + k) % 4) for k in range(1, 4)]
    peers += [at(l=(l + k) % 4) for k in range(1, 4)]
    for peer in peers:
        pl.semaphore_signal(barrier, inc=1, device_id=peer, device_id_type=MESH)
    for n in range(6):
        fetch(n).start()
    total[...] = jnp.zeros_like(total)
    grads[...] = jnp.zeros_like(grads)
    fetch(0).wait()
    pl.semaphore_wait(barrier, len(peers))

    for s in range(2):
        rows = pl.ds(s * PART, PART)
        remote(ring.at[0, z, rows], ring.at[1, z, rows], h_send.at[s], ring_recv.at[1, z, s], partner).start()

    def place(q, o):
        dist = (o + 1) // 2
        zf = (z + 8 - dist) % 8 if o % 2 else (z + dist) % 8
        hf = h if q == 0 else 1 - h
        return dist, zf, 2 * hf + zf // 4, zf % 4

    def relay(q, o):
        dist, zf, xf, lf = place(q, o)
        for s in range(2):
            rows = pl.ds(s * PART, PART)
            piece = ring.at[q, zf, rows]
            if (q, o) != (0, 0):
                landed(piece, ring_recv.at[q, zf, s])
            if o == 0 or (o % 2 == 1 and dist + 1 <= 4 - s):
                remote(piece, piece, ring_send.at[q, 0, dist, s], ring_recv.at[q, zf, s], right).start()
            if o == 0 or (o % 2 == 0 and dist + 1 <= 3 + s):
                remote(piece, piece, ring_send.at[q, 1, dist, s], ring_recv.at[q, zf, s], left).start()

            @pl.when(xf != x)
            def _():
                there = blocks.at[lf, x, pl.ds(c * HALF + s * PART, PART)]
                remote(piece, there, x_send.at[q, o, s], x_recv.at[lf, x, s], at(x=xf)).start()

        @pl.when(xf == x)
        def _():
            there = blocks.at[lf, x, pl.ds(c * HALF, HALF)]
            remote(ring.at[q, zf], there, sib_send.at[lf, x], sib_recv.at[lf, x], sibling).start()
            blocks[lf, x, pl.ds(c * HALF, HALF)] = ring[q, zf]

    def share(lf):
        for k in range(1, 4):
            xt = (x + k) % 4
            for s in range(2):
                landed(blocks.at[lf, xt, pl.ds(c * HALF + s * PART, PART)], x_recv.at[lf, xt, s])
            mine = blocks.at[lf, xt, pl.ds(c * HALF, HALF)]
            remote(mine, mine, sib_send.at[lf, xt], sib_recv.at[lf, xt], sibling).start()

    def send_weight(origin, way):
        block = weights.at[origin]
        target = at(l=l + 1) if way == 0 else at(l=l - 1)
        return remote(block, block, w_send.at[way, origin], w_recv.at[origin], target)

    def pass_weight(step):
        @pl.when(l >= step)
        def _():
            if step:
                landed(weights.at[l - step], w_recv.at[l - step])

            @pl.when(l < 3)
            def _():
                send_weight(l - step, 0).start()

        @pl.when(l + step <= 3)
        def _():
            if step:
                landed(weights.at[l + step], w_recv.at[l + step])

            @pl.when(l > 0)
            def _():
                send_weight(l + step, 1).start()

    def project_pair():
        fetch(1).wait()
        fetch(2).wait()
        product = jnp.dot(inputs[...], projector[...], preferred_element_type=F32)
        part[...] = product.T.reshape(part.shape)
        remote(part.at[:, :, 1 - c], part_in, p_send, p_recv, sibling).start()

    def project_half():
        landed(part_in, p_recv)
        pair[...] = part[:, :, c] + part_in[...]
        half_out[...] = pair[1 - h].astype(BF16)
        remote(half_out, half_in, ph_send, ph_recv, partner).start()

    def project_share():
        landed(half_in, ph_recv)
        pair[h] = pair[h] + half_in[...].astype(F32)
        shares[...] = pair[h].astype(BF16)
        for k in range(1, 8):
            zp = (z + k) % 8
            remote(shares.at[zp], shares_in.at[z], pz_send.at[zp], pz_recv.at[z], at(z=zp)).start()

    def project_own():
        own = pair[h, z]
        for k in range(1, 8):
            zp = (z + k) % 8
            landed(shares_in.at[zp], pz_recv.at[zp])
            own = own + shares_in[zp].astype(F32)
        projected[x] = own.astype(BF16)
        for k in range(1, 4):
            xp = (x + k) % 4
            remote(projected.at[x], projected.at[x], px_send.at[xp], px_recv.at[x], at(x=xp)).start()

    for n, (q, o) in enumerate(ORDER):
        relay(q, o)
        if n == 0:
            project_pair()
        if n == 1:
            project_half()
        if n == 3:
            project_share()
        if n == 4:
            fetch(3).wait()
            pass_weight(0)
        if n == 6:
            project_own()
        if n == 9:
            pass_weight(1)
        if n == 14:
            pass_weight(2)

    for k in range(1, 4):
        xp = (x + k) % 4
        landed(projected.at[xp], px_recv.at[xp])

    @pl.when(l == 3)
    def _():
        landed(weights.at[0], w_recv.at[0])

    @pl.when(l == 0)
    def _():
        landed(weights.at[3], w_recv.at[3])

    def multiply(o, carry):
        dist = (o + 1) // 2
        zf = (z + jnp.where(o % 2 == 1, 8 - dist, dist)) % 8
        lf = zf % 4

        @pl.when(zf // 4 == x % 2)
        def _():
            share(lf)

            def add(k, carry):
                xt = (x + k) % 4
                landed(blocks.at[lf, xt, pl.ds((1 - c) * HALF, HALF)], sib_recv.at[lf, xt])
                block = blocks[lf, xt]
                grads[lf] += lax.dot_general(
                    projected[xt], block, (((1,), (1,)), ((), ())), preferred_element_type=F32
                )
                total[xt] += jnp.dot(weights[lf], block, preferred_element_type=F32)
                return carry

            lax.fori_loop(0, 4, add, 0)

            @pl.when(lf != l)
            def _():
                grads_out[lf] = grads[lf].astype(BF16)
                remote(grads_out.at[lf], grads_in.at[l], g_send.at[lf], g_recv.at[l], at(l=lf)).start()

        return carry

    lax.fori_loop(0, 8, multiply, 0)

    for k in range(1, 4):
        xp = (x + k) % 4
        sums_out[xp] = total[xp].astype(BF16)
        remote(sums_out.at[xp], sums_in.at[x], c_send.at[xp], c_recv.at[x], at(x=xp)).start()

    fetch(4).wait()
    fetch(5).wait()
    gradient = grads[l]
    for k in range(1, 4):
        lp = (l + k) % 4
        landed(grads_in.at[lp], g_recv.at[lp])
        gradient = gradient + grads_in[lp].astype(F32)
    moment_one = decay_first * first[...] + (1.0 - decay_first) * gradient
    moment_two = decay_second * second[...] + (1.0 - decay_second) * gradient * gradient
    direction[h, z, c] = (
        moment_one / bias_first / (jnp.sqrt(moment_two / bias_second) + epsilon_value)
    ).astype(BF16)

    mine = direction.at[h, z, c]
    remote(mine, mine, dh_send, d_recv.at[1, z], partner).start()
    for q, o in ORDER:
        dist, zf, _, _ = place(q, o)
        hf = h if q == 0 else 1 - h
        piece = direction.at[hf, zf, c]
        if (q, o) != (0, 0):
            landed(piece, d_recv.at[q, zf])
        if o == 0 or (o % 2 == 1 and dist + 1 <= 4 - q):
            remote(piece, piece, d_send.at[q, 0, dist], d_recv.at[q, zf], right).start()
        if o == 0 or (o % 2 == 0 and dist + 1 <= 3 + q):
            remote(piece, piece, d_send.at[q, 1, dist], d_recv.at[q, zf], left).start()
    both = direction.at[:, :, c]
    remote(both, both, ds_send, ds_recv, sibling).start()

    result = total[x]
    for k in range(1, 4):
        xp = (x + k) % 4
        landed(sums_in.at[xp], c_recv.at[xp])
        result = result + sums_in[xp].astype(F32)
    grad_out[...] = result.T.astype(BF16)

    landed(direction.at[:, :, 1 - c], ds_recv)
    update_out[...] = jnp.dot(
        projector[...], direction[...].reshape(512, 896), preferred_element_type=F32
    ).astype(BF16)

    for s in range(2):
        landed(ring.at[0, z, pl.ds(s * PART, PART)], h_send.at[s])
    for q, o in ORDER:
        dist, zf, xf, lf = place(q, o)
        for s in range(2):
            piece = ring.at[q, zf, pl.ds(s * PART, PART)]
            if o == 0 or (o % 2 == 1 and dist + 1 <= 4 - s):
                landed(piece, ring_send.at[q, 0, dist, s])
            if o == 0 or (o % 2 == 0 and dist + 1 <= 3 + s):
                landed(piece, ring_send.at[q, 1, dist, s])

            @pl.when(xf != x)
            def _():
                landed(piece, x_send.at[q, o, s])

        if o == 0 or (o % 2 == 1 and dist + 1 <= 4 - q):
            landed(direction.at[h, zf, c], d_send.at[q, 0, dist])
        if o == 0 or (o % 2 == 0 and dist + 1 <= 3 + q):
            landed(direction.at[h, zf, c], d_send.at[q, 1, dist])
    for lf in range(4):
        for xt in range(4):
            landed(blocks.at[lf, xt, pl.ds(c * HALF, HALF)], sib_send.at[lf, xt])
    for step in range(3):

        @pl.when((l >= step) & (l < 3))
        def _():
            send_weight(l - step, 0).wait_send()

        @pl.when((l + step <= 3) & (l > 0))
        def _():
            send_weight(l + step, 1).wait_send()

    landed(part_in, p_send)
    landed(half_out, ph_send)
    for k in range(1, 8):
        zp = (z + k) % 8
        landed(shares.at[zp], pz_send.at[zp])
    for k in range(1, 4):
        xp, lp = (x + k) % 4, (l + k) % 4
        landed(projected.at[x], px_send.at[xp])
        landed(grads_out.at[lp], g_send.at[lp])
        landed(sums_out.at[xp], c_send.at[xp])
    landed(mine, dh_send)
    landed(both, ds_send)


def body(inputs, cotangent, weight, projector, first_moment, second_moment):
    dma = pltpu.SemaphoreType.DMA
    vmem = pl.BlockSpec(memory_space=pltpu.VMEM)
    return pl.pallas_call(
        kernel,
        out_shape=(
            jax.ShapeDtypeStruct((256, 256), BF16),
            jax.ShapeDtypeStruct((256, 896), BF16),
        ),
        in_specs=[pl.BlockSpec(memory_space=pltpu.HBM)] * 6,
        out_specs=(vmem, vmem),
        scratch_shapes=[
            pltpu.VMEM((256, 256), BF16),
            pltpu.VMEM((256, 512), BF16),
            pltpu.VMEM((16, 896), F32),
            pltpu.VMEM((16, 896), F32),
            pltpu.VMEM((2, 8, 448, 256), BF16),
            pltpu.VMEM((4, 4, 896, 256), BF16),
            pltpu.VMEM((4, 256, 896), BF16),
            pltpu.VMEM((4, 256, 256), F32),
            pltpu.VMEM((4, 16, 896), F32),
            pltpu.VMEM((2, 8, 2, 16, 256), F32),
            pltpu.VMEM((2, 8, 16, 256), F32),
            pltpu.VMEM((2, 8, 16, 256), F32),
            pltpu.VMEM((8, 16, 256), BF16),
            pltpu.VMEM((8, 16, 256), BF16),
            pltpu.VMEM((8, 16, 256), BF16),
            pltpu.VMEM((8, 16, 256), BF16),
            pltpu.VMEM((4, 16, 256), BF16),
            pltpu.VMEM((4, 16, 896), BF16),
            pltpu.VMEM((4, 16, 896), BF16),
            pltpu.VMEM((4, 256, 256), BF16),
            pltpu.VMEM((4, 256, 256), BF16),
            pltpu.VMEM((2, 8, 2, 16, 896), BF16),
            dma((6,)), dma((2,)), dma((2, 8, 2)), dma((2, 2, 4, 2)), dma((2, 8, 2)), dma((4, 4, 2)),
            dma((4, 4)), dma((4, 4)), dma((2, 4)), dma((4,)),
            dma(()), dma(()), dma(()), dma(()), dma((8,)), dma((8,)), dma((4,)), dma((4,)),
            dma((4,)), dma((4,)), dma((4,)), dma((4,)), dma(()), dma((2, 8)), dma((2, 2, 4)), dma(()), dma(()),
        ],
        compiler_params=pltpu.CompilerParams(
            collective_id=0, has_side_effects=True, vmem_limit_bytes=56000 * 1024
        ),
        cost_estimate=pl.CostEstimate(
            flops=2_300_000_000, bytes_accessed=2_000_000, transcendentals=28_672
        ),
        name="step",
    )(inputs, cotangent.T, weight, projector, first_moment, second_moment)


def solution(mesh):
    return jax.shard_map(
        body,
        mesh=mesh,
        in_specs=(
            P("fsdp", "dp"),
            P("fsdp", "dp"),
            P("dp", "fsdp"),
            P("dp", None),
            P("dp", "fsdp"),
            P("dp", "fsdp"),
        ),
        out_specs=(P("fsdp", "dp"), P("dp", "fsdp")),
        check_vma=False,
    )
```

```python
import jax
import jax.numpy as jnp
from jax import lax
from jax.experimental import pallas as pl
from jax.experimental.pallas import tpu as pltpu
from jax.sharding import PartitionSpec as P

decay_first = 0.9
decay_second = 0.999
bias_first = 0.9999734386
bias_second = 0.0952078528
epsilon_value = 1e-08

MESH = pl.DeviceIdType.MESH
BF16 = jnp.bfloat16
F32 = jnp.float32

ORDER = (
    (0, 0), (0, 1), (0, 2), (0, 3), (1, 0), (0, 4), (1, 1), (1, 2), (0, 5), (1, 3), (1, 4), (0, 6), (1, 5), (1, 6), (0, 7), (1, 7),
)
FIRST = ((0, 2), (0, -2), (1, 0), (1, 2), (1, -2), (0, 1), (0, -1))
PASS = (
    (0, -2, (1, 2)), (0, 2, (-1,)), (1, 0, (1, -1)), (1, -2, (1,)), (1, 2, (-1, -2)),
)
HALF = 448
PART = 224


def remote(src, dst, send, recv, device):
    return pltpu.make_async_remote_copy(
        src_ref=src,
        dst_ref=dst,
        send_sem=send,
        recv_sem=recv,
        device_id=device,
        device_id_type=MESH,
    )


def landed(ref, sem):
    pltpu.make_async_copy(ref, ref, sem).wait()


def kernel(
    inputs_hbm, cotangent_hbm, weight_hbm, projector_hbm, first_hbm, second_hbm, grad_out, update_out,
    inputs, projector, first, second, ring, blocks, weights, total, grads, part, part_in, pair, half_out, half_in, shares, shares_in, projected,
    grads_out, grads_in, sums_out, sums_in, direction,
    load, h_send, ring_recv, ring_send, x_send, x_recv, sib_send, sib_recv, w_send, w_recv,
    p_send, p_recv, ph_send, ph_recv, pz_send, pz_recv, px_send, px_recv,
    g_send, g_recv, c_send, c_recv, d_recv, d_send, d_pass, ds_send, ds_recv,
):
    j = lax.axis_index("dp")
    i = lax.axis_index("fsdp")
    x, l = i // 4, i % 4
    h, z, c = j // 16, (j // 2) % 8, j % 2

    def at(x=x, l=l, h=h, z=z, c=c):
        return {"dp": h * 16 + z * 2 + c, "fsdp": x * 4 + l}

    sibling = at(c=1 - c)
    partner = at(h=1 - h)
    right, left = at(z=(z + 1) % 8), at(z=(z + 7) % 8)

    def fetch(n):
        src, dst = (
            (cotangent_hbm, ring.at[0, z]), (inputs_hbm, inputs), (projector_hbm, projector),
            (weight_hbm, weights.at[l]), (first_hbm, first), (second_hbm, second),
        )[n]
        return pltpu.make_async_copy(src, dst, load.at[n])

    barrier = pltpu.get_barrier_semaphore()
    peers = [sibling, partner]
    peers += [at(z=(z + k) % 8) for k in range(1, 8)]
    peers += [at(h=1 - h, z=(z + k) % 8) for k in (2, 6)]
    peers += [at(x=(x + k) % 4) for k in range(1, 4)]
    peers += [at(l=(l + k) % 4) for k in range(1, 4)]
    for peer in peers:
        pl.semaphore_signal(barrier, inc=1, device_id=peer, device_id_type=MESH)
    for n in range(6):
        fetch(n).start()
    total[...] = jnp.zeros_like(total)
    grads[...] = jnp.zeros_like(grads)
    fetch(0).wait()
    pl.semaphore_wait(barrier, len(peers))

    for s in range(2):
        rows = pl.ds(s * PART, PART)
        remote(ring.at[0, z, rows], ring.at[1, z, rows], h_send.at[s], ring_recv.at[1, z, s], partner).start()

    def place(q, o):
        dist = (o + 1) // 2
        zf = (z + 8 - dist) % 8 if o % 2 else (z + dist) % 8
        hf = h if q == 0 else 1 - h
        return dist, zf, 2 * hf + zf // 4, zf % 4

    def relay(q, o):
        dist, zf, xf, lf = place(q, o)
        for s in range(2):
            rows = pl.ds(s * PART, PART)
            piece = ring.at[q, zf, rows]
            if (q, o) != (0, 0):
                landed(piece, ring_recv.at[q, zf, s])
            if o == 0 or (o % 2 == 1 and dist + 1 <= 4 - s):
                remote(piece, piece, ring_send.at[q, 0, dist, s], ring_recv.at[q, zf, s], right).start()
            if o == 0 or (o % 2 == 0 and dist + 1 <= 3 + s):
                remote(piece, piece, ring_send.at[q, 1, dist, s], ring_recv.at[q, zf, s], left).start()

            @pl.when(xf != x)
            def _():
                there = blocks.at[lf, x, pl.ds(c * HALF + s * PART, PART)]
                remote(piece, there, x_send.at[q, o, s], x_recv.at[lf, x, s], at(x=xf)).start()

        @pl.when(xf == x)
        def _():
            there = blocks.at[lf, x, pl.ds(c * HALF, HALF)]
            remote(ring.at[q, zf], there, sib_send.at[lf, x], sib_recv.at[lf, x], sibling).start()
            blocks[lf, x, pl.ds(c * HALF, HALF)] = ring[q, zf]

    def share(lf):
        for k in range(1, 4):
            xt = (x + k) % 4
            for s in range(2):
                landed(blocks.at[lf, xt, pl.ds(c * HALF + s * PART, PART)], x_recv.at[lf, xt, s])
            mine = blocks.at[lf, xt, pl.ds(c * HALF, HALF)]
            remote(mine, mine, sib_send.at[lf, xt], sib_recv.at[lf, xt], sibling).start()

    def send_weight(origin, way):
        block = weights.at[origin]
        target = at(l=l + 1) if way == 0 else at(l=l - 1)
        return remote(block, block, w_send.at[way, origin], w_recv.at[origin], target)

    def pass_weight(step):
        @pl.when(l >= step)
        def _():
            if step:
                landed(weights.at[l - step], w_recv.at[l - step])

            @pl.when(l < 3)
            def _():
                send_weight(l - step, 0).start()

        @pl.when(l + step <= 3)
        def _():
            if step:
                landed(weights.at[l + step], w_recv.at[l + step])

            @pl.when(l > 0)
            def _():
                send_weight(l + step, 1).start()

    def project_pair():
        fetch(1).wait()
        fetch(2).wait()
        product = jnp.dot(inputs[...], projector[...], preferred_element_type=F32)
        part[...] = product.T.reshape(part.shape)
        remote(part.at[:, :, 1 - c], part_in, p_send, p_recv, sibling).start()

    def project_half():
        landed(part_in, p_recv)
        pair[...] = part[:, :, c] + part_in[...]
        half_out[...] = pair[1 - h].astype(BF16)
        remote(half_out, half_in, ph_send, ph_recv, partner).start()

    def project_share():
        landed(half_in, ph_recv)
        pair[h] = pair[h] + half_in[...].astype(F32)
        shares[...] = pair[h].astype(BF16)
        for k in range(1, 8):
            zp = (z + k) % 8
            remote(shares.at[zp], shares_in.at[z], pz_send.at[zp], pz_recv.at[z], at(z=zp)).start()

    def project_own():
        own = pair[h, z]
        for k in range(1, 8):
            zp = (z + k) % 8
            landed(shares_in.at[zp], pz_recv.at[zp])
            own = own + shares_in[zp].astype(F32)
        projected[x] = own.astype(BF16)
        for k in range(1, 4):
            xp = (x + k) % 4
            remote(projected.at[x], projected.at[x], px_send.at[xp], px_recv.at[x], at(x=xp)).start()

    for n, (q, o) in enumerate(ORDER):
        relay(q, o)
        if n == 0:
            project_pair()
        if n == 2:
            project_half()
        if n == 7:
            project_share()
        if n == 4:
            fetch(3).wait()
            pass_weight(0)
        if n == 11:
            project_own()
        if n == 9:
            pass_weight(1)
        if n == 14:
            pass_weight(2)

    for k in range(1, 4):
        xp = (x + k) % 4
        landed(projected.at[xp], px_recv.at[xp])

    @pl.when(l == 3)
    def _():
        landed(weights.at[0], w_recv.at[0])

    @pl.when(l == 0)
    def _():
        landed(weights.at[3], w_recv.at[3])

    def multiply(o, carry):
        dist = (o + 1) // 2
        zf = (z + jnp.where(o % 2 == 1, 8 - dist, dist)) % 8
        lf = zf % 4

        @pl.when(zf // 4 == x % 2)
        def _():
            share(lf)

            def add(k, carry):
                xt = (x + k) % 4
                landed(blocks.at[lf, xt, pl.ds((1 - c) * HALF, HALF)], sib_recv.at[lf, xt])
                block = blocks[lf, xt]
                grads[lf] += lax.dot_general(
                    projected[xt], block, (((1,), (1,)), ((), ())), preferred_element_type=F32
                )
                total[xt] += jnp.dot(weights[lf], block, preferred_element_type=F32)
                return carry

            lax.fori_loop(0, 4, add, 0)

            @pl.when(lf != l)
            def _():
                grads_out[lf] = grads[lf].astype(BF16)
                remote(grads_out.at[lf], grads_in.at[l], g_send.at[lf], g_recv.at[l], at(l=lf)).start()

        return carry

    lax.fori_loop(0, 8, multiply, 0)

    for k in range(1, 4):
        xp = (x + k) % 4
        sums_out[xp] = total[xp].astype(BF16)
        remote(sums_out.at[xp], sums_in.at[x], c_send.at[xp], c_recv.at[x], at(x=xp)).start()

    fetch(4).wait()
    fetch(5).wait()
    gradient = grads[l]
    for k in range(1, 4):
        lp = (l + k) % 4
        landed(grads_in.at[lp], g_recv.at[lp])
        gradient = gradient + grads_in[lp].astype(F32)
    moment_one = decay_first * first[...] + (1.0 - decay_first) * gradient
    moment_two = decay_second * second[...] + (1.0 - decay_second) * gradient * gradient
    direction[h, z, c] = (
        moment_one / bias_first / (jnp.sqrt(moment_two / bias_second) + epsilon_value)
    ).astype(BF16)

    def hand_on(q, offset, steps):
        hf = h if q == 0 else 1 - h
        zf = (z + 8 + offset) % 8
        piece = direction.at[hf, zf, c]
        landed(piece, d_recv.at[q, zf])
        for step in steps:
            target = at(z=(z + 8 + step) % 8)
            remote(piece, piece, d_pass.at[q, offset + 2, step + 2], d_recv.at[q, zf], target).start()

    mine = direction.at[h, z, c]
    for n, (q, step) in enumerate(FIRST):
        target = at(h=h if q == 0 else 1 - h, z=(z + 8 + step) % 8)
        remote(mine, mine, d_send.at[n], d_recv.at[q, z], target).start()
    for q, offset, steps in PASS:
        hand_on(q, offset, steps)
    for q in range(2):
        for offset in (-4, -3, -1, 1, 3):
            hand_on(q, offset, ())
    both = direction.at[:, :, c]
    remote(both, both, ds_send, ds_recv, sibling).start()

    result = total[x]
    for k in range(1, 4):
        xp = (x + k) % 4
        landed(sums_in.at[xp], c_recv.at[xp])
        result = result + sums_in[xp].astype(F32)
    grad_out[...] = result.T.astype(BF16)

    landed(direction.at[:, :, 1 - c], ds_recv)
    update_out[...] = jnp.dot(
        projector[...], direction[...].reshape(512, 896), preferred_element_type=F32
    ).astype(BF16)

    for s in range(2):
        landed(ring.at[0, z, pl.ds(s * PART, PART)], h_send.at[s])
    for q, o in ORDER:
        dist, zf, xf, lf = place(q, o)
        for s in range(2):
            piece = ring.at[q, zf, pl.ds(s * PART, PART)]
            if o == 0 or (o % 2 == 1 and dist + 1 <= 4 - s):
                landed(piece, ring_send.at[q, 0, dist, s])
            if o == 0 or (o % 2 == 0 and dist + 1 <= 3 + s):
                landed(piece, ring_send.at[q, 1, dist, s])

            @pl.when(xf != x)
            def _():
                landed(piece, x_send.at[q, o, s])
    for lf in range(4):
        for xt in range(4):
            landed(blocks.at[lf, xt, pl.ds(c * HALF, HALF)], sib_send.at[lf, xt])
    for step in range(3):

        @pl.when((l >= step) & (l < 3))
        def _():
            send_weight(l - step, 0).wait_send()

        @pl.when((l + step <= 3) & (l > 0))
        def _():
            send_weight(l + step, 1).wait_send()

    landed(part_in, p_send)
    landed(half_out, ph_send)
    for k in range(1, 8):
        zp = (z + k) % 8
        landed(shares.at[zp], pz_send.at[zp])
    for k in range(1, 4):
        xp, lp = (x + k) % 4, (l + k) % 4
        landed(projected.at[x], px_send.at[xp])
        landed(grads_out.at[lp], g_send.at[lp])
        landed(sums_out.at[xp], c_send.at[xp])
    for n in range(len(FIRST)):
        landed(mine, d_send.at[n])
    for q, offset, steps in PASS:
        for step in steps:
            landed(mine, d_pass.at[q, offset + 2, step + 2])
    landed(both, ds_send)


def body(inputs, cotangent, weight, projector, first_moment, second_moment):
    dma = pltpu.SemaphoreType.DMA
    vmem = pl.BlockSpec(memory_space=pltpu.VMEM)
    return pl.pallas_call(
        kernel,
        out_shape=(
            jax.ShapeDtypeStruct((256, 256), BF16),
            jax.ShapeDtypeStruct((256, 896), BF16),
        ),
        in_specs=[pl.BlockSpec(memory_space=pltpu.HBM)] * 6,
        out_specs=(vmem, vmem),
        scratch_shapes=[
            pltpu.VMEM((256, 256), BF16),
            pltpu.VMEM((256, 512), BF16),
            pltpu.VMEM((16, 896), F32),
            pltpu.VMEM((16, 896), F32),
            pltpu.VMEM((2, 8, 448, 256), BF16),
            pltpu.VMEM((4, 4, 896, 256), BF16),
            pltpu.VMEM((4, 256, 896), BF16),
            pltpu.VMEM((4, 256, 256), F32),
            pltpu.VMEM((4, 16, 896), F32),
            pltpu.VMEM((2, 8, 2, 16, 256), F32),
            pltpu.VMEM((2, 8, 16, 256), F32),
            pltpu.VMEM((2, 8, 16, 256), F32),
            pltpu.VMEM((8, 16, 256), BF16),
            pltpu.VMEM((8, 16, 256), BF16),
            pltpu.VMEM((8, 16, 256), BF16),
            pltpu.VMEM((8, 16, 256), BF16),
            pltpu.VMEM((4, 16, 256), BF16),
            pltpu.VMEM((4, 16, 896), BF16),
            pltpu.VMEM((4, 16, 896), BF16),
            pltpu.VMEM((4, 256, 256), BF16),
            pltpu.VMEM((4, 256, 256), BF16),
            pltpu.VMEM((2, 8, 2, 16, 896), BF16),
            dma((6,)), dma((2,)), dma((2, 8, 2)), dma((2, 2, 4, 2)), dma((2, 8, 2)), dma((4, 4, 2)),
            dma((4, 4)), dma((4, 4)), dma((2, 4)), dma((4,)),
            dma(()), dma(()), dma(()), dma(()), dma((8,)), dma((8,)), dma((4,)), dma((4,)),
            dma((4,)), dma((4,)), dma((4,)), dma((4,)), dma((2, 8)), dma((7,)), dma((2, 5, 5)), dma(()), dma(()),
        ],
        compiler_params=pltpu.CompilerParams(
            collective_id=0, has_side_effects=True, vmem_limit_bytes=56000 * 1024
        ),
        cost_estimate=pl.CostEstimate(
            flops=2_300_000_000, bytes_accessed=2_000_000, transcendentals=28_672
        ),
        name="step",
    )(inputs, cotangent.T, weight, projector, first_moment, second_moment)


def solution(mesh):
    return jax.shard_map(
        body,
        mesh=mesh,
        in_specs=(
            P("fsdp", "dp"),
            P("fsdp", "dp"),
            P("dp", "fsdp"),
            P("dp", None),
            P("dp", "fsdp"),
            P("dp", "fsdp"),
        ),
        out_specs=(P("fsdp", "dp"), P("dp", "fsdp")),
        check_vma=False,
    )
```

```python
import jax
import jax.numpy as jnp
from jax import lax
from jax.experimental import pallas as pl
from jax.experimental.pallas import tpu as pltpu
from jax.sharding import PartitionSpec as P

decay_first = 0.9
decay_second = 0.999
bias_first = 0.9999734386
bias_second = 0.0952078528
epsilon_value = 1e-08

MESH = pl.DeviceIdType.MESH
BF16 = jnp.bfloat16
F32 = jnp.float32

ORDER = (
    (0, 0), (0, 1), (1, 0), (1, 1), (0, 2), (1, 2), (0, 3), (1, 3), (0, 4), (1, 4),
)
FIRST = ((0, 2), (0, -2), (1, 0), (1, 2), (1, -2), (0, 1), (0, -1))
PASS = (
    (0, -2, (1, 2)), (0, 2, (-1,)), (1, 0, (1, -1)), (1, -2, (1,)), (1, 2, (-1, -2)),
)
HALF = 448
PARTS = 4
PART = HALF // PARTS


def remote(src, dst, send, recv, device):
    return pltpu.make_async_remote_copy(
        src_ref=src,
        dst_ref=dst,
        send_sem=send,
        recv_sem=recv,
        device_id=device,
        device_id_type=MESH,
    )


def landed(ref, sem):
    pltpu.make_async_copy(ref, ref, sem).wait()


def kernel(
    inputs_hbm, cotangent_hbm, weight_hbm, projector_hbm, first_hbm, second_hbm, grad_out, update_out,
    inputs, projector, first, second, ring, blocks, weights, total, grads, part, part_in, pair, half_out, half_in, shares, shares_in, projected,
    grads_out, grads_in, sums_out, sums_in, direction,
    load, h_send, ring_recv, ring_send, x_send, x_recv, sib_send, sib_recv, w_send, w_recv,
    p_send, p_recv, ph_send, ph_recv, pz_send, pz_recv, px_send, px_recv,
    g_send, g_recv, c_send, c_recv, d_recv, d_send, d_pass, ds_send, ds_recv,
):
    j = lax.axis_index("dp")
    i = lax.axis_index("fsdp")
    x, l = i // 4, i % 4
    h, z, c = j // 16, (j // 2) % 8, j % 2

    def at(x=x, l=l, h=h, z=z, c=c):
        return {"dp": h * 16 + z * 2 + c, "fsdp": x * 4 + l}

    sibling = at(c=1 - c)
    partner = at(h=1 - h)
    right, left = at(z=(z + 1) % 8), at(z=(z + 7) % 8)

    def fetch(n):
        src, dst = (
            (cotangent_hbm, ring.at[0, z]), (inputs_hbm, inputs), (projector_hbm, projector),
            (weight_hbm, weights.at[l]), (first_hbm, first), (second_hbm, second),
        )[n]
        return pltpu.make_async_copy(src, dst, load.at[n])

    barrier = pltpu.get_barrier_semaphore()
    peers = [sibling, partner]
    peers += [at(z=(z + k) % 8) for k in range(1, 8)]
    peers += [at(h=1 - h, z=(z + k) % 8) for k in (2, 6)]
    peers += [at(x=(x + k) % 4) for k in range(1, 4)]
    peers += [at(l=(l + k) % 4) for k in range(1, 4)]
    for peer in peers:
        pl.semaphore_signal(barrier, inc=1, device_id=peer, device_id_type=MESH)
    for n in range(6):
        fetch(n).start()
    total[...] = jnp.zeros_like(total)
    grads[...] = jnp.zeros_like(grads)
    fetch(0).wait()
    pl.semaphore_wait(barrier, len(peers))

    for s in range(PARTS):
        rows = pl.ds(s * PART, PART)
        remote(ring.at[0, z, rows], ring.at[1, z, rows], h_send.at[s], ring_recv.at[1, z, s], partner).start()

    def arrivals(q, dist):
        hf = h if q == 0 else 1 - h
        for s in range(PARTS):
            limit = (4, 3) if s % 2 == 0 else (3, 4)
            for way in range(2):
                if dist > limit[way] or (dist == 0 and way == 1):
                    continue
                zf = (z + 8 - dist) % 8 if way == 0 else (z + dist) % 8
                ways = (0, 1) if dist == 0 else (way,) if dist < limit[way] else ()
                yield zf, 2 * hf + zf // 4, s, 2 * dist - way, ways

    def relay(q, dist):
        for zf, xf, s, o, ways in arrivals(q, dist):
            piece = ring.at[q, zf, pl.ds(s * PART, PART)]
            if (q, dist) != (0, 0):
                landed(piece, ring_recv.at[q, zf, s])
            for way in ways:
                remote(piece, piece, ring_send.at[q, way, dist, s], ring_recv.at[q, zf, s], (right, left)[way]).start()

            @pl.when(xf != x)
            def _():
                there = blocks.at[zf % 4, x, pl.ds(c * HALF + s * PART, PART)]
                remote(piece, there, x_send.at[q, o, s], x_recv.at[zf % 4, x, s], at(x=xf)).start()

        for zf in {0: [z], 4: [(z + 4) % 8]}.get(dist, [(z + 8 - dist) % 8, (z + dist) % 8]):
            lf, xf = zf % 4, 2 * (h if q == 0 else 1 - h) + zf // 4

            @pl.when(xf == x)
            def _():
                there = blocks.at[lf, x, pl.ds(c * HALF, HALF)]
                remote(ring.at[q, zf], there, sib_send.at[lf, x], sib_recv.at[lf, x], sibling).start()
                blocks[lf, x, pl.ds(c * HALF, HALF)] = ring[q, zf]

    def share(lf):
        for k in range(1, 4):
            xt = (x + k) % 4
            for s in range(PARTS):
                landed(blocks.at[lf, xt, pl.ds(c * HALF + s * PART, PART)], x_recv.at[lf, xt, s])
            mine = blocks.at[lf, xt, pl.ds(c * HALF, HALF)]
            remote(mine, mine, sib_send.at[lf, xt], sib_recv.at[lf, xt], sibling).start()

    def send_weight(origin, way):
        block = weights.at[origin]
        target = at(l=l + 1) if way == 0 else at(l=l - 1)
        return remote(block, block, w_send.at[way, origin], w_recv.at[origin], target)

    def pass_weight(step):
        @pl.when(l >= step)
        def _():
            if step:
                landed(weights.at[l - step], w_recv.at[l - step])

            @pl.when(l < 3)
            def _():
                send_weight(l - step, 0).start()

        @pl.when(l + step <= 3)
        def _():
            if step:
                landed(weights.at[l + step], w_recv.at[l + step])

            @pl.when(l > 0)
            def _():
                send_weight(l + step, 1).start()

    def project_pair():
        fetch(1).wait()
        fetch(2).wait()
        product = jnp.dot(inputs[...], projector[...], preferred_element_type=F32)
        part[...] = product.T.reshape(part.shape)
        remote(part.at[:, :, 1 - c], part_in, p_send, p_recv, sibling).start()

    def project_half():
        landed(part_in, p_recv)
        pair[...] = part[:, :, c] + part_in[...]
        half_out[...] = pair[1 - h].astype(BF16)
        remote(half_out, half_in, ph_send, ph_recv, partner).start()

    def project_share():
        landed(half_in, ph_recv)
        pair[h] = pair[h] + half_in[...].astype(F32)
        shares[...] = pair[h].astype(BF16)
        for k in range(1, 8):
            zp = (z + k) % 8
            remote(shares.at[zp], shares_in.at[z], pz_send.at[zp], pz_recv.at[z], at(z=zp)).start()

    def project_own():
        own = pair[h, z]
        for k in range(1, 8):
            zp = (z + k) % 8
            landed(shares_in.at[zp], pz_recv.at[zp])
            own = own + shares_in[zp].astype(F32)
        projected[x] = own.astype(BF16)
        for k in range(1, 4):
            xp = (x + k) % 4
            remote(projected.at[x], projected.at[x], px_send.at[xp], px_recv.at[x], at(x=xp)).start()

    for n, (q, dist) in enumerate(ORDER):
        relay(q, dist)
        if n == 0:
            project_pair()
        if n == 1:
            project_half()
        if n == 4:
            project_share()
        if n == 2:
            fetch(3).wait()
            pass_weight(0)
        if n == 7:
            project_own()
        if n == 5:
            pass_weight(1)
        if n == 8:
            pass_weight(2)

    for k in range(1, 4):
        xp = (x + k) % 4
        landed(projected.at[xp], px_recv.at[xp])

    @pl.when(l == 3)
    def _():
        landed(weights.at[0], w_recv.at[0])

    @pl.when(l == 0)
    def _():
        landed(weights.at[3], w_recv.at[3])

    def multiply(lf):
        def add(k, carry):
            xt = (x + k) % 4
            landed(blocks.at[lf, xt, pl.ds((1 - c) * HALF, HALF)], sib_recv.at[lf, xt])
            block = blocks[lf, xt]
            grads[lf] += lax.dot_general(
                projected[xt], block, (((1,), (1,)), ((), ())), preferred_element_type=F32
            )
            total[xt] += jnp.dot(weights[lf], block, preferred_element_type=F32)
            return carry

        lax.fori_loop(0, 4, add, 0)

        @pl.when(lf != l)
        def _():
            grads_out[lf] = grads[lf].astype(BF16)
            remote(grads_out.at[lf], grads_in.at[l], g_send.at[lf], g_recv.at[l], at(l=lf)).start()

    def take(o, before):
        dist = (o + 1) // 2
        zf = (z + jnp.where(o % 2 == 1, 8 - dist, dist)) % 8
        lf, mine = zf % 4, zf // 4 == x % 2

        @pl.when(mine)
        def _():
            share(lf)

        @pl.when(mine & (before >= 0))
        def _():
            multiply(before)

        return jnp.where(mine, lf, before)

    multiply(lax.fori_loop(0, 8, take, jnp.int32(-1)))

    for k in range(1, 4):
        xp = (x + k) % 4
        sums_out[xp] = total[xp].astype(BF16)
        remote(sums_out.at[xp], sums_in.at[x], c_send.at[xp], c_recv.at[x], at(x=xp)).start()

    fetch(4).wait()
    fetch(5).wait()
    gradient = grads[l]
    for k in range(1, 4):
        lp = (l + k) % 4
        landed(grads_in.at[lp], g_recv.at[lp])
        gradient = gradient + grads_in[lp].astype(F32)
    moment_one = decay_first * first[...] + (1.0 - decay_first) * gradient
    moment_two = decay_second * second[...] + (1.0 - decay_second) * gradient * gradient
    direction[h, z, c] = (
        moment_one / bias_first / (jnp.sqrt(moment_two / bias_second) + epsilon_value)
    ).astype(BF16)

    def hand_on(q, offset, steps):
        hf = h if q == 0 else 1 - h
        zf = (z + 8 + offset) % 8
        piece = direction.at[hf, zf, c]
        landed(piece, d_recv.at[q, zf])
        for step in steps:
            target = at(z=(z + 8 + step) % 8)
            remote(piece, piece, d_pass.at[q, offset + 2, step + 2], d_recv.at[q, zf], target).start()

    mine = direction.at[h, z, c]
    for n, (q, step) in enumerate(FIRST):
        target = at(h=h if q == 0 else 1 - h, z=(z + 8 + step) % 8)
        remote(mine, mine, d_send.at[n], d_recv.at[q, z], target).start()
    for q, offset, steps in PASS:
        hand_on(q, offset, steps)
    for q in range(2):
        for offset in (-4, -3, -1, 1, 3):
            hand_on(q, offset, ())
    both = direction.at[:, :, c]
    remote(both, both, ds_send, ds_recv, sibling).start()

    result = total[x]
    for k in range(1, 4):
        xp = (x + k) % 4
        landed(sums_in.at[xp], c_recv.at[xp])
        result = result + sums_in[xp].astype(F32)
    grad_out[...] = result.T.astype(BF16)

    landed(direction.at[:, :, 1 - c], ds_recv)
    update_out[...] = jnp.dot(
        projector[...], direction[...].reshape(512, 896), preferred_element_type=F32
    ).astype(BF16)

    for s in range(PARTS):
        landed(ring.at[0, z, pl.ds(s * PART, PART)], h_send.at[s])
    for q, dist in ORDER:
        for zf, xf, s, o, ways in arrivals(q, dist):
            piece = ring.at[q, zf, pl.ds(s * PART, PART)]
            for way in ways:
                landed(piece, ring_send.at[q, way, dist, s])

            @pl.when(xf != x)
            def _():
                landed(piece, x_send.at[q, o, s])

    for lf in range(4):
        for xt in range(4):
            landed(blocks.at[lf, xt, pl.ds(c * HALF, HALF)], sib_send.at[lf, xt])
    for step in range(3):

        @pl.when((l >= step) & (l < 3))
        def _():
            send_weight(l - step, 0).wait_send()

        @pl.when((l + step <= 3) & (l > 0))
        def _():
            send_weight(l + step, 1).wait_send()

    landed(part_in, p_send)
    landed(half_out, ph_send)
    for k in range(1, 8):
        zp = (z + k) % 8
        landed(shares.at[zp], pz_send.at[zp])
    for k in range(1, 4):
        xp, lp = (x + k) % 4, (l + k) % 4
        landed(projected.at[x], px_send.at[xp])
        landed(grads_out.at[lp], g_send.at[lp])
        landed(sums_out.at[xp], c_send.at[xp])
    for n in range(len(FIRST)):
        landed(mine, d_send.at[n])
    for q, offset, steps in PASS:
        for step in steps:
            landed(mine, d_pass.at[q, offset + 2, step + 2])
    landed(both, ds_send)


def body(inputs, cotangent, weight, projector, first_moment, second_moment):
    dma = pltpu.SemaphoreType.DMA
    vmem = pl.BlockSpec(memory_space=pltpu.VMEM)
    return pl.pallas_call(
        kernel,
        out_shape=(
            jax.ShapeDtypeStruct((256, 256), BF16),
            jax.ShapeDtypeStruct((256, 896), BF16),
        ),
        in_specs=[pl.BlockSpec(memory_space=pltpu.HBM)] * 6,
        out_specs=(vmem, vmem),
        scratch_shapes=[
            pltpu.VMEM((256, 256), BF16),
            pltpu.VMEM((256, 512), BF16),
            pltpu.VMEM((16, 896), F32),
            pltpu.VMEM((16, 896), F32),
            pltpu.VMEM((2, 8, 448, 256), BF16),
            pltpu.VMEM((4, 4, 896, 256), BF16),
            pltpu.VMEM((4, 256, 896), BF16),
            pltpu.VMEM((4, 256, 256), F32),
            pltpu.VMEM((4, 16, 896), F32),
            pltpu.VMEM((2, 8, 2, 16, 256), F32),
            pltpu.VMEM((2, 8, 16, 256), F32),
            pltpu.VMEM((2, 8, 16, 256), F32),
            pltpu.VMEM((8, 16, 256), BF16),
            pltpu.VMEM((8, 16, 256), BF16),
            pltpu.VMEM((8, 16, 256), BF16),
            pltpu.VMEM((8, 16, 256), BF16),
            pltpu.VMEM((4, 16, 256), BF16),
            pltpu.VMEM((4, 16, 896), BF16),
            pltpu.VMEM((4, 16, 896), BF16),
            pltpu.VMEM((4, 256, 256), BF16),
            pltpu.VMEM((4, 256, 256), BF16),
            pltpu.VMEM((2, 8, 2, 16, 896), BF16),
            dma((6,)), dma((PARTS,)), dma((2, 8, PARTS)), dma((2, 2, 4, PARTS)), dma((2, 9, PARTS)), dma((4, 4, PARTS)),
            dma((4, 4)), dma((4, 4)), dma((2, 4)), dma((4,)),
            dma(()), dma(()), dma(()), dma(()), dma((8,)), dma((8,)), dma((4,)), dma((4,)),
            dma((4,)), dma((4,)), dma((4,)), dma((4,)), dma((2, 8)), dma((7,)), dma((2, 5, 5)), dma(()), dma(()),
        ],
        compiler_params=pltpu.CompilerParams(
            collective_id=0, has_side_effects=True, vmem_limit_bytes=56000 * 1024
        ),
        cost_estimate=pl.CostEstimate(
            flops=2_300_000_000, bytes_accessed=2_000_000, transcendentals=28_672
        ),
        name="step",
    )(inputs, cotangent.T, weight, projector, first_moment, second_moment)


def solution(mesh):
    return jax.shard_map(
        body,
        mesh=mesh,
        in_specs=(
            P("fsdp", "dp"),
            P("fsdp", "dp"),
            P("dp", "fsdp"),
            P("dp", None),
            P("dp", "fsdp"),
            P("dp", "fsdp"),
        ),
        out_specs=(P("fsdp", "dp"), P("dp", "fsdp")),
        check_vma=False,
    )
```

```python
import jax
import jax.numpy as jnp
from jax import lax
from jax.experimental import pallas as pl
from jax.experimental.pallas import tpu as pltpu
from jax.sharding import PartitionSpec as P

decay_first = 0.9
decay_second = 0.999
bias_first = 0.9999734386
bias_second = 0.0952078528
epsilon_value = 1e-08

MESH = pl.DeviceIdType.MESH
BF16 = jnp.bfloat16
F32 = jnp.float32

ORDER = (
    (0, 0), (0, 1), (1, 0), (1, 1), (0, 2), (1, 2), (0, 3), (1, 3), (0, 4), (1, 4),
)
FIRST = ((0, 2), (0, -2), (1, 0), (1, 2), (1, -2), (0, 1), (0, -1))
PASS = (
    (0, -2, (1, 2)), (0, 2, (-1,)), (1, 0, (1, -1)), (1, -2, (1,)), (1, 2, (-1, -2)),
)
HALF = 448
PARTS = 4
PART = HALF // PARTS


def remote(src, dst, send, recv, device):
    return pltpu.make_async_remote_copy(
        src_ref=src,
        dst_ref=dst,
        send_sem=send,
        recv_sem=recv,
        device_id=device,
        device_id_type=MESH,
    )


def landed(ref, sem):
    pltpu.make_async_copy(ref, ref, sem).wait()


def kernel(
    inputs_hbm, cotangent_hbm, weight_hbm, projector_hbm, first_hbm, second_hbm, grad_out, direction_out,
    inputs, projector, first, second, ring, blocks, weights, total, grads, part, part_in, pair, half_out, half_in, shares, shares_in, projected,
    grads_out, grads_in, sums_out, sums_in, direction,
    load, h_send, ring_recv, ring_send, x_send, x_recv, sib_send, sib_recv, w_send, w_recv,
    p_send, p_recv, ph_send, ph_recv, pz_send, pz_recv, px_send, px_recv,
    g_send, g_recv, c_send, c_recv, d_recv, d_send, d_pass, ds_send, ds_recv, store,
):
    j = lax.axis_index("dp")
    i = lax.axis_index("fsdp")
    x, l = i // 4, i % 4
    h, z, c = j // 16, (j // 2) % 8, j % 2

    def at(x=x, l=l, h=h, z=z, c=c):
        return {"dp": h * 16 + z * 2 + c, "fsdp": x * 4 + l}

    sibling = at(c=1 - c)
    partner = at(h=1 - h)
    right, left = at(z=(z + 1) % 8), at(z=(z + 7) % 8)

    def fetch(n):
        src, dst = (
            (cotangent_hbm, ring.at[0, z]), (inputs_hbm, inputs), (projector_hbm, projector),
            (weight_hbm, weights.at[l]), (first_hbm, first), (second_hbm, second),
        )[n]
        return pltpu.make_async_copy(src, dst, load.at[n])

    barrier = pltpu.get_barrier_semaphore()
    peers = [sibling, partner]
    peers += [at(z=(z + k) % 8) for k in range(1, 8)]
    peers += [at(h=1 - h, z=(z + k) % 8) for k in (2, 6)]
    peers += [at(x=(x + k) % 4) for k in range(1, 4)]
    peers += [at(l=(l + k) % 4) for k in range(1, 4)]
    for peer in peers:
        pl.semaphore_signal(barrier, inc=1, device_id=peer, device_id_type=MESH)
    for n in range(6):
        fetch(n).start()
    total[...] = jnp.zeros_like(total)
    grads[...] = jnp.zeros_like(grads)
    fetch(0).wait()
    pl.semaphore_wait(barrier, len(peers))

    for s in range(PARTS):
        rows = pl.ds(s * PART, PART)
        remote(ring.at[0, z, rows], ring.at[1, z, rows], h_send.at[s], ring_recv.at[1, z, s], partner).start()

    def arrivals(q, dist):
        hf = h if q == 0 else 1 - h
        for s in range(PARTS):
            limit = (4, 3) if s % 2 == 0 else (3, 4)
            for way in range(2):
                if dist > limit[way] or (dist == 0 and way == 1):
                    continue
                zf = (z + 8 - dist) % 8 if way == 0 else (z + dist) % 8
                ways = (0, 1) if dist == 0 else (way,) if dist < limit[way] else ()
                yield zf, 2 * hf + zf // 4, s, 2 * dist - way, ways

    def relay(q, dist):
        for zf, xf, s, o, ways in arrivals(q, dist):
            piece = ring.at[q, zf, pl.ds(s * PART, PART)]
            if (q, dist) != (0, 0):
                landed(piece, ring_recv.at[q, zf, s])
            for way in ways:
                remote(piece, piece, ring_send.at[q, way, dist, s], ring_recv.at[q, zf, s], (right, left)[way]).start()

            @pl.when(xf != x)
            def _():
                there = blocks.at[zf % 4, x, pl.ds(c * HALF + s * PART, PART)]
                remote(piece, there, x_send.at[q, o, s], x_recv.at[zf % 4, x, s], at(x=xf)).start()

        for zf in {0: [z], 4: [(z + 4) % 8]}.get(dist, [(z + 8 - dist) % 8, (z + dist) % 8]):
            lf, xf = zf % 4, 2 * (h if q == 0 else 1 - h) + zf // 4

            @pl.when(xf == x)
            def _():
                there = blocks.at[lf, x, pl.ds(c * HALF, HALF)]
                remote(ring.at[q, zf], there, sib_send.at[lf, x], sib_recv.at[lf, x], sibling).start()
                blocks[lf, x, pl.ds(c * HALF, HALF)] = ring[q, zf]

    def share(lf):
        for k in range(1, 4):
            xt = (x + k) % 4
            for s in range(PARTS):
                landed(blocks.at[lf, xt, pl.ds(c * HALF + s * PART, PART)], x_recv.at[lf, xt, s])
            mine = blocks.at[lf, xt, pl.ds(c * HALF, HALF)]
            remote(mine, mine, sib_send.at[lf, xt], sib_recv.at[lf, xt], sibling).start()

    def send_weight(origin, way):
        block = weights.at[origin]
        target = at(l=l + 1) if way == 0 else at(l=l - 1)
        return remote(block, block, w_send.at[way, origin], w_recv.at[origin], target)

    def pass_weight(step):
        @pl.when(l >= step)
        def _():
            if step:
                landed(weights.at[l - step], w_recv.at[l - step])

            @pl.when(l < 3)
            def _():
                send_weight(l - step, 0).start()

        @pl.when(l + step <= 3)
        def _():
            if step:
                landed(weights.at[l + step], w_recv.at[l + step])

            @pl.when(l > 0)
            def _():
                send_weight(l + step, 1).start()

    def project_pair():
        fetch(1).wait()
        fetch(2).wait()
        product = jnp.dot(inputs[...], projector[...], preferred_element_type=F32)
        part[...] = product.T.reshape(part.shape)
        remote(part.at[:, :, 1 - c], part_in, p_send, p_recv, sibling).start()

    def project_half():
        landed(part_in, p_recv)
        pair[...] = part[:, :, c] + part_in[...]
        half_out[...] = pair[1 - h].astype(BF16)
        remote(half_out, half_in, ph_send, ph_recv, partner).start()

    def project_share():
        landed(half_in, ph_recv)
        pair[h] = pair[h] + half_in[...].astype(F32)
        shares[...] = pair[h].astype(BF16)
        for k in range(1, 8):
            zp = (z + k) % 8
            remote(shares.at[zp], shares_in.at[z], pz_send.at[zp], pz_recv.at[z], at(z=zp)).start()

    def project_own():
        own = pair[h, z]
        for k in range(1, 8):
            zp = (z + k) % 8
            landed(shares_in.at[zp], pz_recv.at[zp])
            own = own + shares_in[zp].astype(F32)
        projected[x] = own.astype(BF16)
        for k in range(1, 4):
            xp = (x + k) % 4
            remote(projected.at[x], projected.at[x], px_send.at[xp], px_recv.at[x], at(x=xp)).start()

    for n, (q, dist) in enumerate(ORDER):
        relay(q, dist)
        if n == 0:
            project_pair()
        if n == 1:
            project_half()
        if n == 4:
            project_share()
        if n == 2:
            fetch(3).wait()
            pass_weight(0)
        if n == 7:
            project_own()
        if n == 5:
            pass_weight(1)
        if n == 8:
            pass_weight(2)

    for k in range(1, 4):
        xp = (x + k) % 4
        landed(projected.at[xp], px_recv.at[xp])

    @pl.when(l == 3)
    def _():
        landed(weights.at[0], w_recv.at[0])

    @pl.when(l == 0)
    def _():
        landed(weights.at[3], w_recv.at[3])

    def multiply(lf):
        def add(k, carry):
            xt = (x + k) % 4
            landed(blocks.at[lf, xt, pl.ds((1 - c) * HALF, HALF)], sib_recv.at[lf, xt])
            block = blocks[lf, xt]
            grads[lf] += lax.dot_general(
                projected[xt], block, (((1,), (1,)), ((), ())), preferred_element_type=F32
            )
            return carry

        lax.fori_loop(0, 4, add, 0)

        @pl.when(lf != l)
        def _():
            grads_out[lf] = grads[lf].astype(BF16)
            remote(grads_out.at[lf], grads_in.at[l], g_send.at[lf], g_recv.at[l], at(l=lf)).start()

        def add_total(xt, carry):
            total[xt] += jnp.dot(weights[lf], blocks[lf, xt], preferred_element_type=F32)
            return carry

        lax.fori_loop(0, 4, add_total, 0)

    def take(o, before):
        dist = (o + 1) // 2
        zf = (z + jnp.where(o % 2 == 1, 8 - dist, dist)) % 8
        lf, mine = zf % 4, zf // 4 == x % 2

        @pl.when(mine)
        def _():
            share(lf)

        @pl.when(mine & (before >= 0))
        def _():
            multiply(before)

        return jnp.where(mine, lf, before)

    multiply(lax.fori_loop(0, 8, take, jnp.int32(-1)))

    for k in range(1, 4):
        xp = (x + k) % 4
        sums_out[xp] = total[xp].astype(BF16)
        remote(sums_out.at[xp], sums_in.at[x], c_send.at[xp], c_recv.at[x], at(x=xp)).start()

    fetch(4).wait()
    fetch(5).wait()
    gradient = grads[l]
    for k in range(1, 4):
        lp = (l + k) % 4
        landed(grads_in.at[lp], g_recv.at[lp])
        gradient = gradient + grads_in[lp].astype(F32)
    moment_one = decay_first * first[...] + (1.0 - decay_first) * gradient
    moment_two = decay_second * second[...] + (1.0 - decay_second) * gradient * gradient
    direction[h, z, c] = (
        moment_one / bias_first / (jnp.sqrt(moment_two / bias_second) + epsilon_value)
    ).astype(BF16)

    def hand_on(q, offset, steps):
        hf = h if q == 0 else 1 - h
        zf = (z + 8 + offset) % 8
        piece = direction.at[hf, zf, c]
        landed(piece, d_recv.at[q, zf])
        for step in steps:
            target = at(z=(z + 8 + step) % 8)
            remote(piece, piece, d_pass.at[q, offset + 2, step + 2], d_recv.at[q, zf], target).start()

    mine = direction.at[h, z, c]
    for n, (q, step) in enumerate(FIRST):
        target = at(h=h if q == 0 else 1 - h, z=(z + 8 + step) % 8)
        remote(mine, mine, d_send.at[n], d_recv.at[q, z], target).start()
    for q, offset, steps in PASS:
        hand_on(q, offset, steps)
    for s in range(PARTS):
        landed(ring.at[0, z, pl.ds(s * PART, PART)], h_send.at[s])
    for q, dist in ORDER:
        for zf, xf, s, o, ways in arrivals(q, dist):
            piece = ring.at[q, zf, pl.ds(s * PART, PART)]
            for way in ways:
                landed(piece, ring_send.at[q, way, dist, s])

    for lf in range(4):
        for xt in range(4):
            landed(blocks.at[lf, xt, pl.ds(c * HALF, HALF)], sib_send.at[lf, xt])
    for step in range(3):

        @pl.when((l >= step) & (l < 3))
        def _():
            send_weight(l - step, 0).wait_send()

        @pl.when((l + step <= 3) & (l > 0))
        def _():
            send_weight(l + step, 1).wait_send()

    landed(part_in, p_send)
    landed(half_out, ph_send)
    for k in range(1, 8):
        zp = (z + k) % 8
        landed(shares.at[zp], pz_send.at[zp])
    for q, dist in ORDER:
        for zf, xf, s, o, _ in arrivals(q, dist):

            @pl.when(xf != x)
            def _():
                landed(ring.at[q, zf, pl.ds(s * PART, PART)], x_send.at[q, o, s])

    for q in range(2):
        for offset in (-4, -3, -1, 1, 3):
            hand_on(q, offset, ())
    both = direction.at[:, :, c]
    remote(both, both, ds_send, ds_recv, sibling).start()
    pltpu.make_async_copy(both, direction_out.at[:, :, c], store.at[0]).start()

    result = total[x]
    for k in range(1, 4):
        xp = (x + k) % 4
        landed(sums_in.at[xp], c_recv.at[xp])
        result = result + sums_in[xp].astype(F32)
    grad_out[...] = result.T.astype(BF16)

    other = direction.at[:, :, 1 - c]
    landed(other, ds_recv)
    pltpu.make_async_copy(other, direction_out.at[:, :, 1 - c], store.at[1]).start()
    landed(other, store.at[1])
    landed(both, store.at[0])

    for k in range(1, 4):
        xp, lp = (x + k) % 4, (l + k) % 4
        landed(projected.at[x], px_send.at[xp])
        landed(grads_out.at[lp], g_send.at[lp])
        landed(sums_out.at[xp], c_send.at[xp])
    for n in range(len(FIRST)):
        landed(mine, d_send.at[n])
    for q, offset, steps in PASS:
        for step in steps:
            landed(mine, d_pass.at[q, offset + 2, step + 2])
    landed(both, ds_send)


def finish(grad, projector, direction, grad_out, update_out):
    grad_out[...] = grad[...]
    update_out[...] = jnp.dot(
        projector[...], direction[...].reshape(512, 896), preferred_element_type=F32
    ).astype(BF16)


def body(inputs, cotangent, weight, projector, first_moment, second_moment):
    dma = pltpu.SemaphoreType.DMA
    vmem = pl.BlockSpec(memory_space=pltpu.VMEM)
    grad, direction = pl.pallas_call(
        kernel,
        out_shape=(
            jax.ShapeDtypeStruct((256, 256), BF16),
            jax.ShapeDtypeStruct((2, 8, 2, 16, 896), BF16),
        ),
        in_specs=[pl.BlockSpec(memory_space=pltpu.HBM)] * 6,
        out_specs=(vmem, pl.BlockSpec(memory_space=pltpu.HBM)),
        scratch_shapes=[
            pltpu.VMEM((256, 256), BF16),
            pltpu.VMEM((256, 512), BF16),
            pltpu.VMEM((16, 896), F32),
            pltpu.VMEM((16, 896), F32),
            pltpu.VMEM((2, 8, 448, 256), BF16),
            pltpu.VMEM((4, 4, 896, 256), BF16),
            pltpu.VMEM((4, 256, 896), BF16),
            pltpu.VMEM((4, 256, 256), F32),
            pltpu.VMEM((4, 16, 896), F32),
            pltpu.VMEM((2, 8, 2, 16, 256), F32),
            pltpu.VMEM((2, 8, 16, 256), F32),
            pltpu.VMEM((2, 8, 16, 256), F32),
            pltpu.VMEM((8, 16, 256), BF16),
            pltpu.VMEM((8, 16, 256), BF16),
            pltpu.VMEM((8, 16, 256), BF16),
            pltpu.VMEM((8, 16, 256), BF16),
            pltpu.VMEM((4, 16, 256), BF16),
            pltpu.VMEM((4, 16, 896), BF16),
            pltpu.VMEM((4, 16, 896), BF16),
            pltpu.VMEM((4, 256, 256), BF16),
            pltpu.VMEM((4, 256, 256), BF16),
            pltpu.VMEM((2, 8, 2, 16, 896), BF16),
            dma((6,)), dma((PARTS,)), dma((2, 8, PARTS)), dma((2, 2, 4, PARTS)), dma((2, 9, PARTS)), dma((4, 4, PARTS)),
            dma((4, 4)), dma((4, 4)), dma((2, 4)), dma((4,)),
            dma(()), dma(()), dma(()), dma(()), dma((8,)), dma((8,)), dma((4,)), dma((4,)),
            dma((4,)), dma((4,)), dma((4,)), dma((4,)), dma((2, 8)), dma((7,)), dma((2, 5, 5)), dma(()), dma(()), dma((2,)),
        ],
        compiler_params=pltpu.CompilerParams(
            collective_id=0, has_side_effects=True, vmem_limit_bytes=56000 * 1024
        ),
        cost_estimate=pl.CostEstimate(
            flops=2_300_000_000, bytes_accessed=2_000_000, transcendentals=28_672
        ),
        name="step",
    )(inputs, cotangent.T, weight, projector, first_moment, second_moment)
    return pl.pallas_call(
        finish,
        out_shape=(
            jax.ShapeDtypeStruct((256, 256), BF16),
            jax.ShapeDtypeStruct((256, 896), BF16),
        ),
        in_specs=[vmem] * 3,
        out_specs=(vmem, vmem),
        compiler_params=pltpu.CompilerParams(vmem_limit_bytes=56000 * 1024),
        name="finish",
    )(grad, projector, direction)


def solution(mesh):
    return jax.shard_map(
        body,
        mesh=mesh,
        in_specs=(
            P("fsdp", "dp"),
            P("fsdp", "dp"),
            P("dp", "fsdp"),
            P("dp", None),
            P("dp", "fsdp"),
            P("dp", "fsdp"),
        ),
        out_specs=(P("fsdp", "dp"), P("dp", "fsdp")),
        check_vma=False,
    )
```

```python
import jax
import jax.numpy as jnp
from jax import lax
from jax.experimental import pallas as pl
from jax.experimental.pallas import tpu as pltpu
from jax.sharding import PartitionSpec as P

decay_first = 0.9
decay_second = 0.999
bias_first = 0.9999734386
bias_second = 0.0952078528
epsilon_value = 1e-08

MESH = pl.DeviceIdType.MESH
BF16 = jnp.bfloat16
F32 = jnp.float32

ORDER = (
    (0, 0), (0, 1), (1, 0), (1, 1), (0, 2), (1, 2), (0, 3), (1, 3), (0, 4), (1, 4),
)
FIRST = ((0, 2), (0, -2), (1, 0), (1, 2), (1, -2), (0, 1), (0, -1))
PASS = (
    (0, -2, (1, 2)), (0, 2, (-1,)), (1, 0, (1, -1)), (1, -2, (1,)), (1, 2, (-1, -2)),
)
HALF = 448
PARTS = 4
PART = HALF // PARTS


def remote(src, dst, send, recv, device):
    return pltpu.make_async_remote_copy(
        src_ref=src,
        dst_ref=dst,
        send_sem=send,
        recv_sem=recv,
        device_id=device,
        device_id_type=MESH,
    )


def landed(ref, sem):
    pltpu.make_async_copy(ref, ref, sem).wait()


def kernel(
    inputs_hbm, cotangent_hbm, weight_hbm, projector_hbm, first_hbm, second_hbm, grad_out, direction_out,
    inputs, projector, first, second, ring, blocks, weights, total, grads, part, part_in, pair, half_out, half_in, shares, shares_in, projected,
    grads_out, grads_in, sums_out, sums_in, direction,
    load, h_send, ring_recv, ring_send, x_send, x_recv, sib_send, sib_recv, w_send, w_recv,
    p_send, p_recv, ph_send, ph_recv, pz_send, pz_recv, px_send, px_recv,
    g_send, g_recv, c_send, c_recv, d_recv, d_send, d_pass, ds_send, ds_recv, store,
):
    j = lax.axis_index("dp")
    i = lax.axis_index("fsdp")
    x, l = i // 4, i % 4
    h, z, c = j // 16, (j // 2) % 8, j % 2

    def at(x=x, l=l, h=h, z=z, c=c):
        return {"dp": h * 16 + z * 2 + c, "fsdp": x * 4 + l}

    sibling = at(c=1 - c)
    partner = at(h=1 - h)
    right, left = at(z=(z + 1) % 8), at(z=(z + 7) % 8)

    def fetch(n):
        src, dst = (
            (cotangent_hbm, ring.at[0, z]), (inputs_hbm, inputs), (projector_hbm, projector),
            (weight_hbm, weights.at[l]), (first_hbm, first), (second_hbm, second),
        )[n]
        return pltpu.make_async_copy(src, dst, load.at[n])

    barrier = pltpu.get_barrier_semaphore()
    peers = [sibling, partner]
    peers += [at(z=(z + k) % 8) for k in range(1, 8)]
    peers += [at(h=1 - h, z=(z + k) % 8) for k in (2, 6)]
    peers += [at(x=(x + k) % 4) for k in range(1, 4)]
    peers += [at(l=(l + k) % 4) for k in range(1, 4)]
    for peer in peers:
        pl.semaphore_signal(barrier, inc=1, device_id=peer, device_id_type=MESH)
    for n in range(6):
        fetch(n).start()
    total[...] = jnp.zeros_like(total)
    grads[...] = jnp.zeros_like(grads)
    fetch(0).wait()
    pl.semaphore_wait(barrier, len(peers))

    for s in range(PARTS):
        rows = pl.ds(s * PART, PART)
        remote(ring.at[0, z, rows], ring.at[1, z, rows], h_send.at[s], ring_recv.at[1, z, s], partner).start()

    def arrivals(q, dist):
        hf = h if q == 0 else 1 - h
        for s in range(PARTS):
            limit = (4, 3) if s % 2 == 0 else (3, 4)
            for way in range(2):
                if dist > limit[way] or (dist == 0 and way == 1):
                    continue
                zf = (z + 8 - dist) % 8 if way == 0 else (z + dist) % 8
                ways = (0, 1) if dist == 0 else (way,) if dist < limit[way] else ()
                yield zf, 2 * hf + zf // 4, s, 2 * dist - way, ways

    def relay(q, dist):
        for zf, xf, s, o, ways in arrivals(q, dist):
            piece = ring.at[q, zf, pl.ds(s * PART, PART)]
            if (q, dist) != (0, 0):
                landed(piece, ring_recv.at[q, zf, s])
            for way in ways:
                remote(piece, piece, ring_send.at[q, way, dist, s], ring_recv.at[q, zf, s], (right, left)[way]).start()

            @pl.when(xf != x)
            def _():
                there = blocks.at[zf % 4, x, pl.ds(c * HALF + s * PART, PART)]
                remote(piece, there, x_send.at[q, o, s], x_recv.at[zf % 4, x, s], at(x=xf)).start()

        for zf in {0: [z], 4: [(z + 4) % 8]}.get(dist, [(z + 8 - dist) % 8, (z + dist) % 8]):
            lf, xf = zf % 4, 2 * (h if q == 0 else 1 - h) + zf // 4

            @pl.when(xf == x)
            def _():
                there = blocks.at[lf, x, pl.ds(c * HALF, HALF)]
                remote(ring.at[q, zf], there, sib_send.at[lf, x], sib_recv.at[lf, x], sibling).start()
                blocks[lf, x, pl.ds(c * HALF, HALF)] = ring[q, zf]

    def share(lf):
        for k in range(1, 4):
            xt = (x + k) % 4
            for s in range(PARTS):
                landed(blocks.at[lf, xt, pl.ds(c * HALF + s * PART, PART)], x_recv.at[lf, xt, s])
            mine = blocks.at[lf, xt, pl.ds(c * HALF, HALF)]
            remote(mine, mine, sib_send.at[lf, xt], sib_recv.at[lf, xt], sibling).start()

    def send_weight(origin, way):
        block = weights.at[origin]
        target = at(l=l + 1) if way == 0 else at(l=l - 1)
        return remote(block, block, w_send.at[way, origin], w_recv.at[origin], target)

    def pass_weight(step):
        @pl.when(l >= step)
        def _():
            if step:
                landed(weights.at[l - step], w_recv.at[l - step])

            @pl.when(l < 3)
            def _():
                send_weight(l - step, 0).start()

        @pl.when(l + step <= 3)
        def _():
            if step:
                landed(weights.at[l + step], w_recv.at[l + step])

            @pl.when(l > 0)
            def _():
                send_weight(l + step, 1).start()

    def project_pair():
        fetch(1).wait()
        fetch(2).wait()
        product = jnp.dot(inputs[...], projector[...], preferred_element_type=F32)
        part[...] = product.T.reshape(part.shape)
        remote(part.at[:, :, 1 - c], part_in, p_send, p_recv, sibling).start()

    def project_half():
        landed(part_in, p_recv)
        pair[...] = part[:, :, c] + part_in[...]
        half_out[...] = pair[1 - h].astype(BF16)
        remote(half_out, half_in, ph_send, ph_recv, partner).start()

    def project_share():
        landed(half_in, ph_recv)
        pair[h] = pair[h] + half_in[...].astype(F32)
        shares[...] = pair[h].astype(BF16)
        for k in range(1, 8):
            zp = (z + k) % 8
            remote(shares.at[zp], shares_in.at[z], pz_send.at[zp], pz_recv.at[z], at(z=zp)).start()

    def project_own():
        own = pair[h, z]
        for k in range(1, 8):
            zp = (z + k) % 8
            landed(shares_in.at[zp], pz_recv.at[zp])
            own = own + shares_in[zp].astype(F32)
        projected[x] = own.astype(BF16)
        for k in range(1, 4):
            xp = (x + k) % 4
            remote(projected.at[x], projected.at[x], px_send.at[xp], px_recv.at[x], at(x=xp)).start()

    for n, (q, dist) in enumerate(ORDER):
        relay(q, dist)
        if n == 0:
            project_pair()
        if n == 1:
            project_half()
        if n == 4:
            project_share()
        if n == 2:
            fetch(3).wait()
            pass_weight(0)
        if n == 7:
            project_own()
        if n == 5:
            pass_weight(1)
        if n == 8:
            pass_weight(2)

    for k in range(1, 4):
        xp = (x + k) % 4
        landed(projected.at[xp], px_recv.at[xp])

    @pl.when(l == 3)
    def _():
        landed(weights.at[0], w_recv.at[0])

    @pl.when(l == 0)
    def _():
        landed(weights.at[3], w_recv.at[3])

    def multiply(lf):
        def add(k, carry):
            xt = (x + k) % 4
            landed(blocks.at[lf, xt, pl.ds((1 - c) * HALF, HALF)], sib_recv.at[lf, xt])
            block = blocks[lf, xt]
            grads[lf] += lax.dot_general(
                projected[xt], block, (((1,), (1,)), ((), ())), preferred_element_type=F32
            )
            return carry

        lax.fori_loop(0, 4, add, 0)

        @pl.when(lf != l)
        def _():
            grads_out[lf] = grads[lf].astype(BF16)
            remote(grads_out.at[lf], grads_in.at[l], g_send.at[lf], g_recv.at[l], at(l=lf)).start()

        def add_total(xt, carry):
            total[xt] += jnp.dot(weights[lf], blocks[lf, xt], preferred_element_type=F32)
            return carry

        lax.fori_loop(0, 4, add_total, 0)

    def take(o, before):
        dist = (o + 1) // 2
        zf = (z + jnp.where(o % 2 == 1, 8 - dist, dist)) % 8
        lf, mine = zf % 4, zf // 4 == x % 2

        @pl.when(mine)
        def _():
            share(lf)

        @pl.when(mine & (before >= 0))
        def _():
            multiply(before)

        return jnp.where(mine, lf, before)

    multiply(lax.fori_loop(0, 8, take, jnp.int32(-1)))

    for k in range(1, 4):
        xp = (x + k) % 4
        sums_out[xp] = total[xp].astype(BF16)
        remote(sums_out.at[xp], sums_in.at[x], c_send.at[xp], c_recv.at[x], at(x=xp)).start()

    fetch(4).wait()
    fetch(5).wait()
    gradient = grads[l]
    for k in range(1, 4):
        lp = (l + k) % 4
        landed(grads_in.at[lp], g_recv.at[lp])
        gradient = gradient + grads_in[lp].astype(F32)
    moment_one = decay_first * first[...] + (1.0 - decay_first) * gradient
    moment_two = decay_second * second[...] + (1.0 - decay_second) * gradient * gradient
    direction[h, z, c] = (
        moment_one / bias_first / (jnp.sqrt(moment_two / bias_second) + epsilon_value)
    ).astype(BF16)

    def hand_on(q, offset, steps):
        hf = h if q == 0 else 1 - h
        zf = (z + 8 + offset) % 8
        piece = direction.at[hf, zf, c]
        landed(piece, d_recv.at[q, zf])
        for step in steps:
            target = at(z=(z + 8 + step) % 8)
            remote(piece, piece, d_pass.at[q, offset + 2, step + 2], d_recv.at[q, zf], target).start()

    mine = direction.at[h, z, c]
    for n, (q, step) in enumerate(FIRST):
        target = at(h=h if q == 0 else 1 - h, z=(z + 8 + step) % 8)
        remote(mine, mine, d_send.at[n], d_recv.at[q, z], target).start()
    for q, offset, steps in PASS:
        hand_on(q, offset, steps)
    for s in range(PARTS):
        landed(ring.at[0, z, pl.ds(s * PART, PART)], h_send.at[s])
    for q, dist in ORDER:
        for zf, xf, s, o, ways in arrivals(q, dist):
            piece = ring.at[q, zf, pl.ds(s * PART, PART)]
            for way in ways:
                landed(piece, ring_send.at[q, way, dist, s])

    for lf in range(4):
        for xt in range(4):
            landed(blocks.at[lf, xt, pl.ds(c * HALF, HALF)], sib_send.at[lf, xt])
    for step in range(3):

        @pl.when((l >= step) & (l < 3))
        def _():
            send_weight(l - step, 0).wait_send()

        @pl.when((l + step <= 3) & (l > 0))
        def _():
            send_weight(l + step, 1).wait_send()

    landed(part_in, p_send)
    landed(half_out, ph_send)
    for k in range(1, 8):
        zp = (z + k) % 8
        landed(shares.at[zp], pz_send.at[zp])
    for q, dist in ORDER:
        for zf, xf, s, o, _ in arrivals(q, dist):

            @pl.when(xf != x)
            def _():
                landed(ring.at[q, zf, pl.ds(s * PART, PART)], x_send.at[q, o, s])

    for q in range(2):
        for offset in (-4, -3, -1, 1, 3):
            hand_on(q, offset, ())
        hf = h if q == 0 else 1 - h
        half = direction.at[hf, :, c]
        remote(half, half, ds_send.at[q], ds_recv.at[q], sibling).start()
        pltpu.make_async_copy(half, direction_out.at[hf, :, c], store.at[0, q]).start()
    result = total[x]
    for k in range(1, 4):
        xp = (x + k) % 4
        landed(sums_in.at[xp], c_recv.at[xp])
        result = result + sums_in[xp].astype(F32)
    grad_out[...] = result.T.astype(BF16)

    for q in range(2):
        hf = h if q == 0 else 1 - h
        other = direction.at[hf, :, 1 - c]
        landed(other, ds_recv.at[q])
        pltpu.make_async_copy(other, direction_out.at[hf, :, 1 - c], store.at[1, q]).start()
    for q in range(2):
        for n in range(2):
            landed(direction.at[h, :, c], store.at[n, q])

    for k in range(1, 4):
        xp, lp = (x + k) % 4, (l + k) % 4
        landed(projected.at[x], px_send.at[xp])
        landed(grads_out.at[lp], g_send.at[lp])
        landed(sums_out.at[xp], c_send.at[xp])
    for n in range(len(FIRST)):
        landed(mine, d_send.at[n])
    for q, offset, steps in PASS:
        for step in steps:
            landed(mine, d_pass.at[q, offset + 2, step + 2])
    for q in range(2):
        landed(direction.at[h, :, c], ds_send.at[q])


def finish(grad, projector, direction, grad_out, update_out):
    grad_out[...] = grad[...]
    update_out[...] = jnp.dot(
        projector[...], direction[...].reshape(512, 896), preferred_element_type=F32
    ).astype(BF16)


def body(inputs, cotangent, weight, projector, first_moment, second_moment):
    dma = pltpu.SemaphoreType.DMA
    vmem = pl.BlockSpec(memory_space=pltpu.VMEM)
    grad, direction = pl.pallas_call(
        kernel,
        out_shape=(
            jax.ShapeDtypeStruct((256, 256), BF16),
            jax.ShapeDtypeStruct((2, 8, 2, 16, 896), BF16),
        ),
        in_specs=[pl.BlockSpec(memory_space=pltpu.HBM)] * 6,
        out_specs=(vmem, pl.BlockSpec(memory_space=pltpu.HBM)),
        scratch_shapes=[
            pltpu.VMEM((256, 256), BF16),
            pltpu.VMEM((256, 512), BF16),
            pltpu.VMEM((16, 896), F32),
            pltpu.VMEM((16, 896), F32),
            pltpu.VMEM((2, 8, 448, 256), BF16),
            pltpu.VMEM((4, 4, 896, 256), BF16),
            pltpu.VMEM((4, 256, 896), BF16),
            pltpu.VMEM((4, 256, 256), F32),
            pltpu.VMEM((4, 16, 896), F32),
            pltpu.VMEM((2, 8, 2, 16, 256), F32),
            pltpu.VMEM((2, 8, 16, 256), F32),
            pltpu.VMEM((2, 8, 16, 256), F32),
            pltpu.VMEM((8, 16, 256), BF16),
            pltpu.VMEM((8, 16, 256), BF16),
            pltpu.VMEM((8, 16, 256), BF16),
            pltpu.VMEM((8, 16, 256), BF16),
            pltpu.VMEM((4, 16, 256), BF16),
            pltpu.VMEM((4, 16, 896), BF16),
            pltpu.VMEM((4, 16, 896), BF16),
            pltpu.VMEM((4, 256, 256), BF16),
            pltpu.VMEM((4, 256, 256), BF16),
            pltpu.VMEM((2, 8, 2, 16, 896), BF16),
            dma((6,)), dma((PARTS,)), dma((2, 8, PARTS)), dma((2, 2, 4, PARTS)), dma((2, 9, PARTS)), dma((4, 4, PARTS)),
            dma((4, 4)), dma((4, 4)), dma((2, 4)), dma((4,)),
            dma(()), dma(()), dma(()), dma(()), dma((8,)), dma((8,)), dma((4,)), dma((4,)),
            dma((4,)), dma((4,)), dma((4,)), dma((4,)), dma((2, 8)), dma((7,)), dma((2, 5, 5)), dma((2,)), dma((2,)), dma((2, 2)),
        ],
        compiler_params=pltpu.CompilerParams(
            collective_id=0, has_side_effects=True, vmem_limit_bytes=56000 * 1024
        ),
        cost_estimate=pl.CostEstimate(
            flops=2_300_000_000, bytes_accessed=2_000_000, transcendentals=28_672
        ),
        name="step",
    )(inputs, cotangent.T, weight, projector, first_moment, second_moment)
    return pl.pallas_call(
        finish,
        out_shape=(
            jax.ShapeDtypeStruct((256, 256), BF16),
            jax.ShapeDtypeStruct((256, 896), BF16),
        ),
        in_specs=[vmem] * 3,
        out_specs=(vmem, vmem),
        compiler_params=pltpu.CompilerParams(vmem_limit_bytes=56000 * 1024),
        name="finish",
    )(grad, projector, direction)


def solution(mesh):
    return jax.shard_map(
        body,
        mesh=mesh,
        in_specs=(
            P("fsdp", "dp"),
            P("fsdp", "dp"),
            P("dp", "fsdp"),
            P("dp", None),
            P("dp", "fsdp"),
            P("dp", "fsdp"),
        ),
        out_specs=(P("fsdp", "dp"), P("dp", "fsdp")),
        check_vma=False,
    )
```
